512 devices in a mesh: row: 8 (over x, core), col: 16 (over y, z_lo), depth: 4 (over z_hi).
Axes of the slice: x: 4, y: 8, z: 8 (z_hi: 4, z_lo: 2; z = z_hi * 2 + z_lo), core: 2. Of those that a mesh axis runs over, the one named last changes fastest.
Arguments:
- upstream: float32 [49152, 1024], P(('row', 'col'), 'depth'), may hold values from -6 to 6
- preact: float32 [49152, 1024], P(('row', 'col'), 'depth'), may hold values from -6 to 6
- features: float32 [49152, 1024], P(('col', 'row'), 'depth'), may hold values from -0.02734375 to 0.02734375
- weight: float32 [1024, 1024], P('depth'), may hold values from -0.1875 to 0.1875
- blocks: float32 [8, 16, 32, 128, 128], P('row', 'col'), may hold values from -0.25 to 0.25
- block_pos: int32 [8, 16, 32], P('row', 'col'), may hold values from 0 to 1151, as said below
- block_count: int32 [8, 16], P('row', 'col'), may hold values from 1 to 32, as said below
Outputs:
- grad_features: float32 [49152, 1024], P(('col', 'row'), 'depth')
- grad_weight: float32 [1024, 1024], P(('depth', 'col'))
The draws below stay inside these ranges and needn't reach their ends.
Inputs may be any that keep to these rules, and one draw needn't show every extreme that they name: `block_pos`: within one tile the positions are distinct. `block_count`: every tile of the first tile row has all 32 slots live; other tiles have at most 16.
All inputs are finite; a program needn't handle non-finite values.
Results may differ from the reference program's by a relative error of at most 0.0006.
Values sent between devices are 32-bit elements; how exact they have to be, the bound alone decides.
A program may use at most 64 MiB of HBM per device.

```python
import jax
import jax.numpy as jnp
from jax import lax

F_IN = 1024
F_OUT = 1024
BLK = 128
DEVICE_NODES = 384
NODES = 49152
TILE_ROWS = 6144
TILE_COLS = 3072
TILE_BLOCK_ROWS = 48
BLOCK_COLS = 24
SLOTS = 32
N_ROW = 8
N_COL = 16


def draw_block_pos(key, part):
    key = jax.random.fold_in(key, 11)
    keys = jax.random.split(key, N_ROW * N_COL)

    def pick_slots(tile_key):
        return jax.random.permutation(tile_key, TILE_BLOCK_ROWS * BLOCK_COLS)[:SLOTS]
    picks = jax.vmap(pick_slots)(keys)
    return picks.reshape(N_ROW, N_COL, SLOTS).astype(jnp.int32)


def draw_block_count(key, part):
    key = jax.random.fold_in(key, 23)
    counts = jax.random.randint(key, (N_ROW, N_COL), max(1, SLOTS // 4), SLOTS // 2 + 1)
    first = jnp.arange(N_ROW, dtype=jnp.int32)[:, None] == 0
    return jnp.where(first, SLOTS, counts).astype(jnp.int32)


def shard_levels(key, shape, cuts, least, largest):
    factor_of = 1.0
    for axis_at, parts in cuts:
        steps = jax.random.uniform(jax.random.fold_in(jax.random.fold_in(key, 6), axis_at), (parts,), jnp.float32, least / len(cuts), largest / len(cuts))
        factor_of = factor_of * jnp.repeat(jnp.exp(steps), shape[axis_at] // parts).reshape((-1,) + (1,) * (len(shape) - 1 - axis_at))
    return factor_of


def gaussian(key, shape, deviation, bound, cuts=(), held_as=jnp.bfloat16):
    drawn = deviation * jax.random.normal(key, shape, jnp.float32)
    if cuts:
        drawn = drawn * shard_levels(key, shape, cuts, -0.22, 0.18)
    return jnp.clip(drawn, -bound, bound).astype(held_as)


def setup_inputs(seed: int = 0) -> dict:
    arg_keys = jax.random.split(jax.random.key(seed), 8)
    return {
        "upstream": gaussian(arg_keys[0], (NODES, F_OUT), 1.0, 6.0, ((0, 128), (1, 4)), jnp.float32),
        "preact": gaussian(arg_keys[1], (NODES, F_OUT), 1.0, 6.0, ((0, 128), (1, 4)), jnp.float32),
        "features": gaussian(arg_keys[2], (NODES, F_IN), NODES ** -0.5, 0.02734375, ((0, 128), (1, 4)), jnp.float32),
        "weight": gaussian(arg_keys[3], (F_IN, F_OUT), F_IN ** -0.5, 0.1875, ((0, 4),), jnp.float32),
        "blocks": gaussian(arg_keys[4], (N_ROW, N_COL, SLOTS, BLK, BLK), (BLK * max(1, SLOTS * BLK // (2 * DEVICE_NODES))) ** -0.5, 0.25, ((0, 8), (1, 16)), jnp.float32),
        "block_pos": draw_block_pos(jax.random.fold_in(arg_keys[7], 71), 0),
        "block_count": draw_block_count(jax.random.fold_in(arg_keys[7], 71), 0),
    }


def tile_summand(signal, blocks, block_pos, block_count, tile_row, tile_col):
    rows = lax.dynamic_slice_in_dim(signal, (tile_row * TILE_ROWS).astype(jnp.int32), TILE_ROWS, 0)
    rows = rows.reshape(TILE_BLOCK_ROWS, BLK, F_OUT)
    tiles = blocks[tile_row, tile_col]
    where = block_pos[tile_row, tile_col]
    count = block_count[tile_row, tile_col]
    live = (jnp.arange(SLOTS, dtype=jnp.int32) < count).astype(jnp.float32)
    masked = tiles * live[:, None, None]
    picked = rows[where // BLOCK_COLS]
    contribution = jnp.einsum("kab,kaf->kbf", masked, picked, precision=lax.Precision.HIGHEST)
    empty = jnp.zeros((BLOCK_COLS, BLK, F_OUT), jnp.float32)
    return empty.at[where % BLOCK_COLS].add(contribution).reshape(TILE_COLS, F_OUT)


def reference(upstream, preact, features, weight, blocks, block_pos, block_count):
    signal = upstream * (preact > 0).astype(jnp.float32)

    def one_tile(step, back):
        step = jnp.asarray(step).astype(jnp.int32)
        tile_row = step // N_COL
        tile_col = step % N_COL
        start = (tile_col * TILE_COLS).astype(jnp.int32)
        term = tile_summand(signal, blocks, block_pos, block_count, tile_row, tile_col)
        current = lax.dynamic_slice_in_dim(back, start, TILE_COLS, 0)
        return lax.dynamic_update_slice_in_dim(back, current + term, start, 0)

    back = lax.fori_loop(0, N_ROW * N_COL, one_tile, jnp.zeros((NODES, F_OUT), jnp.float32))
    grad_features = jnp.dot(back, weight.T, precision=lax.Precision.HIGHEST, preferred_element_type=jnp.float32)
    grad_weight = jnp.dot(features.T, back, precision=lax.Precision.HIGHEST, preferred_element_type=jnp.float32)
    return grad_features, grad_weight
```

```python
import functools

import jax
import jax.numpy as jnp
from jax import lax
from jax.experimental import pallas as pl
from jax.experimental.pallas import tpu as pltpu
from jax.sharding import PartitionSpec as P

BLK = 128
Q = 2
F = 128 // Q
MESH = pl.DeviceIdType.MESH
F32 = jnp.float32
BF16 = jnp.bfloat16
NT = (((1,), (1,)), ((), ()))


def split(v):
    hi = v.astype(BF16)
    return hi, (v - hi.astype(F32)).astype(BF16)


def dot(a, b):
    return jnp.dot(a, b, preferred_element_type=F32)


def dot_nt(a, b):
    return lax.dot_general(a, b, NT, preferred_element_type=F32)


def dot3(ah, al, bh, bl, f):
    return f(ah, bh) + f(al, bh) + f(ah, bl)


def kernel(up, pre, tab_v, tab_own, feat_hbm, w_hbm, blk_hbm, gf_out, gw_out,
           turned, peer_tab_v, peer_tab, own_blk, peer_blk, blk_hi, blk_lo, run,
           feat, wv, ft_hi, ft_lo, w_hi, w_lo, gft,
           gw, gw_in, gw_half, gw_yz, gw_fin, *rest):
    sig = rest[:Q]
    part = rest[Q:2 * Q]
    core_in = rest[2 * Q:3 * Q]
    far_in = rest[3 * Q:4 * Q]
    near_in = rest[4 * Q:5 * Q]
    back = rest[5 * Q:6 * Q]
    other = rest[6 * Q:7 * Q]
    (loc, swap_s, swap_r, tab_s, tab_r, blk_s, blk_r, y_s, y_r, core_s, core_r,
     far_s, far_r, near_s, near_r, z_s, z_r, gwr_s, gwr_r, gwy_s, gwy_r, gwf_s, gwf_r) = rest[7 * Q:]

    r = lax.axis_index("row")
    c = lax.axis_index("col")
    zh = lax.axis_index("depth")
    x, k = r // 2, r % 2
    y, zl = c // 2, c % 2
    z = zh * 2 + zl

    def at(dx=0, dk=0, dy=0, dz=0):
        zz = (z + dz + 8) % 8
        return {"row": ((x + dx + 4) % 4) * 2 + (k + dk) % 2,
                "col": ((y + dy + 8) % 8) * 2 + zz % 2, "depth": zz // 2}

    peer = {"row": r, "col": y * 2 + 1 - zl, "depth": zh}
    pending = []

    def copy(src, dst, ssem, rsem, dev):
        return pltpu.make_async_remote_copy(src_ref=src, dst_ref=dst, send_sem=ssem, recv_sem=rsem,
                                            device_id=dev, device_id_type=MESH)

    def send(src, dst, ssem, rsem, dev):
        cp = copy(src, dst, ssem, rsem, dev)
        cp.start()
        pending.append(cp)

    def got(dst, ssem, rsem):
        copy(dst, dst, ssem, rsem, peer).wait_recv()

    bar = pltpu.get_barrier_semaphore()

    def greet(dev):
        pl.semaphore_signal(bar, inc=1, device_id=dev, device_id_type=MESH)

    @pl.loop(1, 8)
    def _(j):
        greet({"row": (r + j) % 8, "col": c, "depth": zh})

    @pl.loop(1, 16)
    def _(j):
        greet({"row": r, "col": (c + j) % 16, "depth": zh})

    out_dz = jnp.where(zl == 0, -1, 1)
    greet(at(dz=out_dz))
    greet(at(dz=2))
    greet(at(dz=-2))

    local = [pltpu.make_async_copy(s, d, loc.at[i]) for i, (s, d) in enumerate(
        ((blk_hbm, own_blk), (feat_hbm, feat), (w_hbm, wv)))]
    for cp in local:
        cp.start()

    for i in range(3):
        for h in range(2):
            u = up[i * BLK:(i + 1) * BLK, h * BLK:(h + 1) * BLK]
            p = pre[i * BLK:(i + 1) * BLK, h * BLK:(h + 1) * BLK]
            turned[h, i] = (u * (p > 0).astype(F32)).T
    for i in range(3):
        v = turned[zl, i]
        for q in range(Q):
            sig[q][6 * y + 3 * zl + i] = v[q * F:(q + 1) * F]

    pl.semaphore_wait(bar, 25)

    n_slots = jnp.where(r == 0, 32, 16)

    def swap_send(q):
        send(turned.at[1 - zl, :, pl.ds(q * F, F)], sig[q].at[pl.ds(6 * y + 3 * zl, 3)],
             swap_s.at[q], swap_r.at[q], peer)

    def swap_wait(q):
        got(sig[q].at[pl.ds(6 * y + 3 * (1 - zl), 3)], swap_s.at[q], swap_r.at[q])

    def y_piece(q, yo, hr):
        h = zl if hr == 0 else 1 - zl
        return sig[q].at[pl.ds(6 * yo + 3 * h, 3)]

    def y_send(q, d, s, hr):
        sgn = 1 - 2 * d
        ref = y_piece(q, (y - sgn * (s - 1) + 8) % 8, hr)
        send(ref, ref, y_s.at[q, d, hr, s - 1], y_r.at[q, d, hr, s - 1], at(dy=sgn))

    def y_first(q, hr):
        for d in range(2):
            y_send(q, d, 1, hr)

    def y_step(q, s, hr):
        for d in range(2):
            last = 4 if d == hr else 3
            if s > last:
                continue
            sgn = 1 - 2 * d
            got(y_piece(q, (y - sgn * s + 8) % 8, hr), y_s.at[q, d, hr, s - 1], y_r.at[q, d, hr, s - 1])
            if s < last:
                y_send(q, d, s + 1, hr)

    def blk_copy(j):
        lo = 8 * j
        return copy(blk_hbm.at[pl.ds(lo, 8)], peer_blk.at[pl.ds(lo, 8)], blk_s.at[j], blk_r.at[j],
                    at(dz=1 if j % 2 == 0 else -1))

    def blk_send():
        send(tab_v, peer_tab_v, tab_s.at[0], tab_r.at[0], peer)
        for j in range(2):
            blk_copy(j).start()

        @pl.when(r == 0)
        def _():
            for j in range(2, 4):
                blk_copy(j).start()

    def blk_wait():
        for j in range(2):
            blk_copy(j).wait_recv()

        @pl.when(r == 0)
        def _():
            for j in range(2, 4):
                blk_copy(j).wait_recv()

    def blk_done():
        for j in range(2):
            blk_copy(j).wait_send()

        @pl.when(r == 0)
        def _():
            for j in range(2, 4):
                blk_copy(j).wait_send()

    def split_blocks(rel):
        src = own_blk if rel == 0 else peer_blk

        @pl.loop(0, n_slots)
        def _(i):
            hi, lo = split(src[i])
            blk_hi[rel, i] = hi
            blk_lo[rel, i] = lo

    def prep_own():
        local[0].wait()
        split_blocks(0)

    def prep_peer():
        got(peer_tab_v, tab_s.at[0], tab_r.at[0])
        cp = pltpu.make_async_copy(peer_tab_v, peer_tab, loc.at[3])
        cp.start()
        blk_wait()
        split_blocks(1)
        cp.wait()

    def prep_feat():
        local[1].wait()
        for i in range(3):
            for h in range(2):
                t = feat[i * BLK:(i + 1) * BLK, h * BLK:(h + 1) * BLK].T
                t = t.reshape(8, 2, 8, BLK)
                for kk in range(2):
                    hi, lo = split(t[:, kk].reshape(64, BLK))
                    row = kk * BLK + h * 64
                    ft_hi[row:row + 64, i * BLK:(i + 1) * BLK] = hi
                    ft_lo[row:row + 64, i * BLK:(i + 1) * BLK] = lo

    def prep_w():
        local[2].wait()
        for q in range(Q):
            v = jnp.concatenate([wv[:, zz * BLK + q * F:zz * BLK + (q + 1) * F] for zz in range(8)], axis=1)
            w_hi[q], w_lo[q] = split(v)

    def spmm(q, rel):
        tab = tab_own if rel == 0 else peer_tab

        def body(it, acc):
            terms = []
            for u in range(4):
                i = it * 4 + u
                sh, sl = split(sig[q][tab[0, i]])
                o = tab[1, i]
                bh, bl = blk_hi[rel, o], blk_lo[rel, o]
                terms.append(dot3(sh, sl, bh, bl, dot) * tab[2, i].astype(F32))
            for u in range(4):
                i = it * 4 + u
                acc = terms[u] + acc * tab[3, i].astype(F32)
                run[i] = acc
            return acc

        lax.fori_loop(0, n_slots // 4, body, jnp.zeros((F, BLK), F32))
        for b in range(24):
            rr = b // 3
            part[q][rr // 2, rr % 2, rel, b % 3] = run[tab[4, b]] * tab[5, b].astype(F32)

    def core_send(q):
        for o in (2, 1, 3, 0):
            xx = (x + o) % 4
            send(part[q].at[xx, 1 - k], core_in[q].at[xx], core_s.at[q, o], core_r.at[q, o], at(dk=1))

    def core_sum(q, o):
        xx = (x + o) % 4
        got(core_in[q].at[xx], core_s.at[q, o], core_r.at[q, o])
        part[q][xx, k] = part[q][xx, k] + core_in[q][xx]

    def x_far(q):
        core_sum(q, 2)
        xx = (x + 2) % 4
        for rel, sgn in ((0, 1), (1, -1)):
            send(part[q].at[xx, k, rel], far_in[q].at[rel], far_s.at[q, rel], far_r.at[q, rel], at(dx=sgn))

    def x_near(q):
        for rel, sgn in ((0, 1), (1, -1)):
            o = sgn % 4
            core_sum(q, o)
            xx = (x + o) % 4
            got(far_in[q].at[rel], far_s.at[q, rel], far_r.at[q, rel])
            part[q][xx, k, rel] = part[q][xx, k, rel] + far_in[q][rel]
            send(part[q].at[xx, k], near_in[q].at[rel], near_s.at[q, rel], near_r.at[q, rel], at(dx=sgn))
        core_sum(q, 0)

    def z_piece(q, dz):
        return back[q].at[pl.ds(((z + dz + 8) % 8) * F, F)]

    def z_start(q):
        for rel in range(2):
            got(near_in[q].at[rel], near_s.at[q, rel], near_r.at[q, rel])
        for rel in range(2):
            for i in range(3):
                v = part[q][x, k, rel, i] + near_in[q][0, rel, i] + near_in[q][1, rel, i]
                if rel == 0:
                    back[q][pl.ds(z * F, F), i * BLK:(i + 1) * BLK] = v
                else:
                    other[q][:, i * BLK:(i + 1) * BLK] = v
        for d, sgn in ((0, 1), (1, -1)):
            send(other[q], z_piece(q, 0), z_s.at[q, d], z_r.at[q, d], at(dz=sgn))
        for d, sgn in ((0, 1), (1, -1)):
            send(z_piece(q, 0), z_piece(q, 0), z_s.at[q, 2 + d], z_r.at[q, 2 + d], at(dz=2 * sgn))

    def z_near(q):
        for d, sgn in ((0, 1), (1, -1)):
            ref = z_piece(q, -sgn)
            got(ref, z_s.at[q, d], z_r.at[q, d])
            send(ref, ref, z_s.at[q, 4 + d], z_r.at[q, 4 + d], at(dz=2 * sgn))

    def z_half(q, dz, d):
        return back[q].at[pl.ds(((z + dz + 8) % 8) * F + d * (F // 2), F // 2)]

    def z_two(q):
        for d, sgn in ((0, 1), (1, -1)):
            got(z_piece(q, -2 * sgn), z_s.at[q, 2 + d], z_r.at[q, 2 + d])
            ref = z_half(q, -2 * sgn, d)
            send(ref, ref, z_s.at[q, 6 + d], z_r.at[q, 6 + d], at(dz=2 * sgn))

    def z_end(q):
        for d, sgn in ((0, 1), (1, -1)):
            got(z_piece(q, -3 * sgn), z_s.at[q, 4 + d], z_r.at[q, 4 + d])
        for d, sgn in ((0, 1), (1, -1)):
            got(z_half(q, -4 * sgn, d), z_s.at[q, 6 + d], z_r.at[q, 6 + d])

    def gemm(q):
        bh, bl = split(back[q][...])
        g = dot3(ft_hi[...], ft_lo[...], bh, bl, dot_nt)
        for xx in range(4):
            gw[q, xx] = g[:, xx * BLK:(xx + 1) * BLK].reshape(2, BLK, BLK)
        gw_send(q)
        t = dot3(w_hi[q], w_lo[q], bh, bl, dot)
        if q == 0:
            gft[...] = t
        elif q < Q - 1:
            gft[...] = gft[...] + t
        else:
            t = gft[...] + t
            for i in range(3):
                for h in range(2):
                    gf_out[i * BLK:(i + 1) * BLK, h * BLK:(h + 1) * BLK] = (
                        t[h * BLK:(h + 1) * BLK, i * BLK:(i + 1) * BLK].T)

    def gw_row(q, j):
        rr = (r + j) % 8
        return copy(gw.at[q, rr // 2, rr % 2], gw_in.at[q, j], gwr_s.at[q, j], gwr_r.at[q, j],
                    {"row": rr, "col": c, "depth": zh})

    def gw_col(q, j):
        cc = (c + j) % 16
        return copy(gw_half.at[q, cc], gw_yz.at[q, j], gwy_s.at[q, j], gwy_r.at[q, j],
                    {"row": r, "col": cc, "depth": zh})

    def gw_all(q, j):
        rr = (r + j) % 8
        return copy(gw_fin.at[q, r], gw_fin.at[q, r], gwf_s.at[q, j], gwf_r.at[q, j],
                    {"row": rr, "col": c, "depth": zh})

    def gw_all_in(q, j):
        ref = gw_fin.at[q, (r - j + 8) % 8]
        return copy(ref, ref, gwf_s.at[q, j], gwf_r.at[q, j], peer)

    def gw_send(q):
        @pl.loop(1, 8)
        def _(j):
            gw_row(q, j).start()

    def gw_sum(q):
        @pl.loop(1, 8)
        def _(j):
            gw_row(q, j).wait_recv()
        v = gw[q, x, k]
        for j in range(1, 8):
            v = v + gw_in[q, j]
        gw_half[q] = v.reshape(16, 8, BLK)

        @pl.loop(1, 16)
        def _(j):
            gw_col(q, j).start()

    def gw_cols(q):
        @pl.loop(1, 16)
        def _(j):
            gw_col(q, j).wait_recv()
        v = gw_half[q, c]
        for j in range(1, 16):
            v = v + gw_yz[q, j]
        gw_fin[q, r] = v

        @pl.loop(1, 8)
        def _(j):
            gw_all(q, j).start()

    def gw_end():
        for q in range(Q):
            @pl.loop(1, 8)
            def _(j):
                gw_all_in(q, j).wait_recv()
        for xx in range(4):
            for kk in range(2):
                for zz in range(2):
                    v = jnp.concatenate([gw_fin[q, 2 * xx + kk][:, zz * F:(zz + 1) * F] for q in range(Q)], axis=1)
                    lane = (2 * xx + zz) * BLK
                    gw_out[kk * 8:(kk + 1) * 8, lane:lane + BLK] = v

    def drain():
        for cp in pending:
            cp.wait_send()
        blk_done()
        for q in range(Q):
            @pl.loop(1, 8)
            def _(j):
                gw_row(q, j).wait_send()
                gw_all(q, j).wait_send()

            @pl.loop(1, 16)
            def _(j):
                gw_col(q, j).wait_send()

    def tail(q):
        return [(spmm, q, 0), (spmm, q, 1), (core_send, q), (x_far, q), (x_near, q),
                (z_start, q), (z_near, q), (z_two, q), (z_end, q), (gemm, q), (gw_sum, q), (gw_cols, q)]

    order = [
        (swap_send, 0), (y_first, 0, 0), (swap_send, 1), (blk_send,), (swap_wait, 0), (y_first, 0, 1),
        (prep_feat,), (y_step, 0, 1, 0), (y_step, 0, 1, 1), (prep_w,), (y_step, 0, 2, 0), (y_step, 0, 2, 1),
        (prep_own,), (y_step, 0, 3, 0), (swap_wait, 1), (y_first, 1, 0), (y_step, 0, 3, 1), (y_first, 1, 1),
        (y_step, 0, 4, 0), (y_step, 0, 4, 1), (prep_peer,),
        (spmm, 0, 0), (y_step, 1, 1, 0), (spmm, 0, 1), (core_send, 0), (y_step, 1, 1, 1), (y_step, 1, 2, 0),
        (x_far, 0), (y_step, 1, 2, 1), (y_step, 1, 3, 0), (x_near, 0), (y_step, 1, 3, 1),
        (y_step, 1, 4, 0), (y_step, 1, 4, 1),
        (spmm, 1, 0), (spmm, 1, 1), (core_send, 1), (z_start, 0),
        (x_far, 1), (z_near, 0), (x_near, 1), (z_two, 0), (z_start, 1), (z_end, 0),
        (gemm, 0), (z_near, 1), (z_two, 1), (gw_sum, 0), (gw_cols, 0), (z_end, 1), (gemm, 1), (gw_sum, 1),
        (gw_cols, 1), (gw_end,), (drain,),
    ]
    for fn, *args in order:
        fn(*args)


def tables(block_pos, block_count):
    n = block_pos.shape[-1]
    pos = block_pos.reshape(n)
    i = jnp.arange(n, dtype=jnp.int32)
    live = (i < block_count.reshape(())).astype(jnp.int32)
    col = jnp.where(live == 1, pos % 24, 24)
    key = col * n + i
    rank = jnp.sum((key[None, :] < key[:, None]).astype(jnp.int32), axis=1)
    hot = (rank[None, :] == i[:, None]).astype(jnp.int32)
    row_s = jnp.sum(hot * (pos // 24)[None, :], axis=1)
    slot_s = jnp.sum(hot * i[None, :], axis=1)
    live_s = jnp.sum(hot * live[None, :], axis=1)
    same = (col[None, :] == col[:, None]).astype(jnp.int32)
    seen = jnp.sum(same * (i[None, :] < i[:, None]).astype(jnp.int32), axis=1)
    cont = jnp.sum(hot * ((seen > 0) & (live == 1)).astype(jnp.int32)[None, :], axis=1)
    b = jnp.arange(24, dtype=jnp.int32)
    at_col = (col[None, :] == b[:, None]).astype(jnp.int32)
    last = jnp.max(at_col * rank[None, :], axis=1)
    has = jnp.max(at_col, axis=1)

    def line(v):
        return jnp.pad(v, (0, BLK - v.shape[0]))[None]

    zero = jnp.zeros((2, BLK), jnp.int32)
    return jnp.concatenate([line(row_s), line(slot_s), line(live_s), line(cont), line(last), line(has), zero])


def body(upstream, preact, features, weight, blocks, block_pos, block_count):
    tab = tables(block_pos, block_count)
    vmem = pl.BlockSpec(memory_space=pltpu.VMEM)
    smem = pl.BlockSpec(memory_space=pltpu.SMEM)
    hbm = pl.BlockSpec(memory_space=pl.ANY)
    dma = pltpu.SemaphoreType.DMA
    V = pltpu.VMEM
    scratch = [
        V((2, 3, BLK, BLK), F32),
        V((8, BLK), jnp.int32),
        pltpu.SMEM((8, BLK), jnp.int32),
        V((32, BLK, BLK), F32), V((32, BLK, BLK), F32),
        V((2, 32, BLK, BLK), BF16), V((2, 32, BLK, BLK), BF16),
        V((32, F, BLK), F32),
        V((384, 256), F32), V((256, 1024), F32),
        V((256, 384), BF16), V((256, 384), BF16),
        V((Q, 256, 8 * F), BF16), V((Q, 256, 8 * F), BF16),
        V((256, 384), F32),
        V((Q, 4, 2, BLK, BLK), F32),
        V((Q, 8, BLK, BLK), F32),
        V((Q, 16, 8, BLK), F32),
        V((Q, 16, 8, BLK), F32),
        V((Q, 8, 8, BLK), F32),
    ]
    for shape in ((48, F, BLK), (4, 2, 2, 3, F, BLK), (4, 2, 3, F, BLK), (2, 3, F, BLK),
                  (2, 2, 3, F, BLK), (8 * F, 384), (F, 384)):
        scratch += [V(shape, F32) for _ in range(Q)]
    scratch += [
        dma((4,)), dma((Q,)), dma((Q,)), dma((1,)), dma((1,)), dma((4,)), dma((4,)),
        dma((Q, 2, 2, 4)), dma((Q, 2, 2, 4)), dma((Q, 4)), dma((Q, 4)),
        dma((Q, 2)), dma((Q, 2)), dma((Q, 2)), dma((Q, 2)), dma((Q, 8)), dma((Q, 8)),
        dma((Q, 8)), dma((Q, 8)), dma((Q, 16)), dma((Q, 16)), dma((Q, 8)), dma((Q, 8)),
    ]
    return pl.pallas_call(
        kernel,
        out_shape=(jax.ShapeDtypeStruct((384, 256), F32), jax.ShapeDtypeStruct((16, 1024), F32)),
        in_specs=[vmem, vmem, vmem, smem, hbm, hbm, hbm],
        out_specs=(vmem, vmem),
        scratch_shapes=scratch,
        compiler_params=pltpu.CompilerParams(
            collective_id=0, has_side_effects=True, vmem_limit_bytes=56 * 2**20),
        cost_estimate=pl.CostEstimate(flops=2 * 10**9, bytes_accessed=6 * 2**20, transcendentals=0),
        name="graph_backward",
    )(upstream, preact, tab, tab, features, weight, blocks.reshape(blocks.shape[2:]))


def solution(mesh):
    in_specs = (
        P(("row", "col"), "depth"),
        P(("row", "col"), "depth"),
        P(("col", "row"), "depth"),
        P("depth", None),
        P("row", "col", None, None, None),
        P("row", "col", None),
        P("row", "col"),
    )
    out_specs = (P(("col", "row"), "depth"), P(("depth", "col"), None))
    return jax.shard_map(body, mesh=mesh, in_specs=in_specs, out_specs=out_specs, check_vma=False)
```

```python
import jax
import jax.numpy as jnp
from jax import lax
from jax.experimental import pallas as pl
from jax.experimental.pallas import tpu as pltpu
from jax.sharding import PartitionSpec as P

BLK = 128
CHUNKS = (64, 64)
Q = len(CHUNKS)
START = tuple(sum(CHUNKS[:q]) for q in range(Q))
MESH = pl.DeviceIdType.MESH
F32 = jnp.float32
BF16 = jnp.bfloat16
NT = (((1,), (1,)), ((), ()))


def split(v):
    hi = v.astype(BF16)
    return hi, (v - hi.astype(F32)).astype(BF16)


def dot(a, b):
    return jnp.dot(a, b, preferred_element_type=F32)


def dot_nt(a, b):
    return lax.dot_general(a, b, NT, preferred_element_type=F32)


def dot3(ah, al, bh, bl, f):
    return f(ah, bh) + f(al, bh) + f(ah, bl)


def down(row):
    return jnp.broadcast_to(row, (BLK, BLK)).T


def tables(pos, count):
    lane = lax.broadcasted_iota(jnp.int32, (1, BLK), 1)
    ii = lax.broadcasted_iota(jnp.int32, (BLK, BLK), 0)
    jj = lax.broadcasted_iota(jnp.int32, (BLK, BLK), 1)
    live = (lane < count).astype(jnp.int32)
    brow = (pos * 2731) >> 16
    col = jnp.where(live > 0, pos - 24 * brow, 24)
    col_i = down(col)
    key = col * BLK + lane
    rank = jnp.sum((down(key) < key).astype(jnp.int32), axis=0, keepdims=True)
    same = (col_i == col).astype(jnp.int32)
    seen = jnp.sum(same * (ii < jj).astype(jnp.int32), axis=0, keepdims=True)
    more = jnp.sum(same * (ii > jj).astype(jnp.int32), axis=0, keepdims=True)
    cont = jnp.where(seen > 0, live, 0)
    rank_i = down(rank)
    hot = (rank_i == jj).astype(jnp.int32)

    def put(v):
        return jnp.sum(hot * v, axis=0, keepdims=True)

    at_col = (col_i == jj).astype(jnp.int32)
    last = jnp.sum(at_col * down(jnp.where(more > 0, 0, rank)), axis=0, keepdims=True)
    has = (jnp.sum(at_col, axis=0, keepdims=True) > 0).astype(jnp.int32)
    return [put(down(brow)), put(ii), put(down(live)), put(down(cont)), last, has]


def kernel(up, pre, pos, count, feat_hbm, w_hbm, blk_hbm, gf_out, gw_out,
           turned, tab_v, tab_own, peer_tab_v, peer_tab, own_blk, peer_blk, blk_hi, blk_lo, run,
           feat, wv, ft_hi, ft_lo, gft, *rest):
    parts = [rest[i * Q:(i + 1) * Q] for i in range(16)]
    (sig, part, core_in, far_in, near_in, back, other, back_hi, back_lo, w_hi, w_lo,
     gw, gw_in, gw_half, gw_yz, gw_fin) = parts
    (loc, swap_s, swap_r, tab_s, tab_r, blk_s, blk_r, y_s, y_r, core_s, core_r,
     far_s, far_r, near_s, near_r, z_s, z_r, gwr_s, gwr_r, gwy_s, gwy_r, gwf_s, gwf_r) = rest[16 * Q:]

    r = lax.axis_index("row")
    c = lax.axis_index("col")
    zh = lax.axis_index("depth")
    x, k = r // 2, r % 2
    y, zl = c // 2, c % 2
    z = zh * 2 + zl

    def at(dx=0, dk=0, dy=0, dz=0):
        zz = (z + dz + 8) % 8
        return {"row": ((x + dx + 4) % 4) * 2 + (k + dk) % 2,
                "col": ((y + dy + 8) % 8) * 2 + zz % 2, "depth": zz // 2}

    peer = {"row": r, "col": y * 2 + 1 - zl, "depth": zh}
    pending = []

    def copy(src, dst, ssem, rsem, dev):
        return pltpu.make_async_remote_copy(src_ref=src, dst_ref=dst, send_sem=ssem, recv_sem=rsem,
                                            device_id=dev, device_id_type=MESH)

    def send(src, dst, ssem, rsem, dev):
        cp = copy(src, dst, ssem, rsem, dev)
        cp.start()
        pending.append(cp)

    def got(dst, ssem, rsem):
        copy(dst, dst, ssem, rsem, peer).wait_recv()

    bar = pltpu.get_barrier_semaphore()
    for dev in (at(dx=1), at(dx=-1), at(dk=1), at(dy=1), at(dy=-1), at(dz=1), at(dz=-1), at(dz=2), at(dz=-2)):
        pl.semaphore_signal(bar, inc=1, device_id=dev, device_id_type=MESH)

    local = [pltpu.make_async_copy(s, d, loc.at[i]) for i, (s, d) in enumerate(
        ((blk_hbm, own_blk), (feat_hbm, feat), (w_hbm, wv)))]
    for cp in local:
        cp.start()

    for i in range(3):
        for h in range(2):
            u = up[i * BLK:(i + 1) * BLK, h * BLK:(h + 1) * BLK]
            p = pre[i * BLK:(i + 1) * BLK, h * BLK:(h + 1) * BLK]
            turned[h, i] = (u * (p > 0).astype(F32)).T
    for i in range(3):
        v = turned[zl, i]
        for q in range(Q):
            sig[q][6 * y + 3 * zl + i] = v[START[q]:START[q] + CHUNKS[q]]

    pl.semaphore_wait(bar, 9)

    n_slots = jnp.where(r == 0, 32, 16)

    def swap_send(q):
        send(turned.at[1 - zl, :, pl.ds(START[q], CHUNKS[q])], sig[q].at[pl.ds(6 * y + 3 * zl, 3)],
             swap_s.at[q], swap_r.at[q], peer)

    def swap_wait(q):
        got(sig[q].at[pl.ds(6 * y + 3 * (1 - zl), 3)], swap_s.at[q], swap_r.at[q])

    def y_piece(q, yo, hr):
        h = zl if hr == 0 else 1 - zl
        return sig[q].at[pl.ds(6 * yo + 3 * h, 3)]

    def y_send(q, d, s, hr):
        sgn = 1 - 2 * d
        ref = y_piece(q, (y - sgn * (s - 1) + 8) % 8, hr)
        send(ref, ref, y_s.at[q, d, hr, s - 1], y_r.at[q, d, hr, s - 1], at(dy=sgn))

    def y_first(q, hr):
        for d in range(2):
            y_send(q, d, 1, hr)

    def y_step(q, s, hr):
        for d in range(2):
            last = 4 if d == hr else 3
            if s > last:
                continue
            sgn = 1 - 2 * d
            got(y_piece(q, (y - sgn * s + 8) % 8, hr), y_s.at[q, d, hr, s - 1], y_r.at[q, d, hr, s - 1])
            if s < last:
                y_send(q, d, s + 1, hr)

    def blk_copy(j):
        lo = 8 * j
        return copy(blk_hbm.at[pl.ds(lo, 8)], peer_blk.at[pl.ds(lo, 8)], blk_s.at[j], blk_r.at[j],
                    at(dz=1 if j % 2 == 0 else -1))

    def tab_make():
        tab_v[...] = jnp.zeros_like(tab_v)
        tab_v[0:1, 0:32] = pos[0]
        for i, v in enumerate(tables(tab_v[0:1], count[0, 0])):
            tab_v[i:i + 1] = v
        send(tab_v, peer_tab_v, tab_s.at[0], tab_r.at[0], peer)
        cp = pltpu.make_async_copy(tab_v, tab_own, loc.at[4])
        cp.start()
        cp.wait()

    def blk_send():
        for j in range(2):
            blk_copy(j).start()

        @pl.when(r == 0)
        def _():
            for j in range(2, 4):
                blk_copy(j).start()

    def blk_wait():
        for j in range(2):
            blk_copy(j).wait_recv()

        @pl.when(r == 0)
        def _():
            for j in range(2, 4):
                blk_copy(j).wait_recv()

    def blk_done():
        for j in range(2):
            blk_copy(j).wait_send()

        @pl.when(r == 0)
        def _():
            for j in range(2, 4):
                blk_copy(j).wait_send()

    def split_blocks(rel):
        src = own_blk if rel == 0 else peer_blk

        @pl.loop(0, n_slots)
        def _(i):
            hi, lo = split(src[i])
            blk_hi[rel, i] = hi
            blk_lo[rel, i] = lo

    def prep_own():
        local[0].wait()
        split_blocks(0)

    def prep_peer():
        got(peer_tab_v, tab_s.at[0], tab_r.at[0])
        cp = pltpu.make_async_copy(peer_tab_v, peer_tab, loc.at[3])
        cp.start()
        blk_wait()
        split_blocks(1)
        cp.wait()

    def prep_feat():
        local[1].wait()
        for i in range(3):
            for h in range(2):
                t = feat[i * BLK:(i + 1) * BLK, h * BLK:(h + 1) * BLK].T
                t = t.reshape(8, 2, 8, BLK)
                for kk in range(2):
                    hi, lo = split(t[:, kk].reshape(64, BLK))
                    row = kk * BLK + h * 64
                    ft_hi[row:row + 64, i * BLK:(i + 1) * BLK] = hi
                    ft_lo[row:row + 64, i * BLK:(i + 1) * BLK] = lo

    def prep_w():
        local[2].wait()
        for q in range(Q):
            lo, n = START[q], CHUNKS[q]
            v = jnp.concatenate([wv[:, zz * BLK + lo:zz * BLK + lo + n] for zz in range(8)], axis=1)
            w_hi[q][...], w_lo[q][...] = split(v)

    def spmm(q, rel):
        tab = tab_own if rel == 0 else peer_tab
        f = CHUNKS[q]

        def step(it, acc):
            terms = []
            for u in range(4):
                i = it * 4 + u
                sh, sl = split(sig[q][tab[0, i]])
                o = tab[1, i]
                t = dot(jnp.concatenate([sh, sl], axis=0), blk_hi[rel, o])
                t = t[:f] + t[f:] + dot(sh, blk_lo[rel, o])
                terms.append(t * tab[2, i].astype(F32))
            for u in range(4):
                i = it * 4 + u
                acc = terms[u] + acc * tab[3, i].astype(F32)
                run[i, 0:f] = acc
            return acc

        lax.fori_loop(0, n_slots // 4, step, jnp.zeros((f, BLK), F32))
        for b in range(24):
            rr = b // 3
            part[q][rr // 2, rr % 2, rel, b % 3] = run[tab[4, b], 0:f] * tab[5, b].astype(F32)

    def core_send(q, rel):
        for o in (2, 1, 3, 0):
            xx = (x + o) % 4
            send(part[q].at[xx, 1 - k, rel], core_in[q].at[xx, rel],
                 core_s.at[q, rel, o], core_r.at[q, rel, o], at(dk=1))

    def core_sum(q, rel, o):
        xx = (x + o) % 4
        got(core_in[q].at[xx, rel], core_s.at[q, rel, o], core_r.at[q, rel, o])
        part[q][xx, k, rel] = part[q][xx, k, rel] + core_in[q][xx, rel]

    def x_far(q, rel):
        core_sum(q, rel, 2)
        xx = (x + 2) % 4
        f = CHUNKS[q] // 2
        for h, sgn in ((0, 1), (1, -1)):
            send(part[q].at[xx, k, rel, :, pl.ds(h * f, f)], far_in[q].at[rel, h],
                 far_s.at[q, rel, h], far_r.at[q, rel, h], at(dx=sgn))

    def x_near(q, rel):
        f = CHUNKS[q] // 2
        for h, sgn in ((0, 1), (1, -1)):
            o = sgn % 4
            core_sum(q, rel, o)
            xx = (x + o) % 4
            got(far_in[q].at[rel, h], far_s.at[q, rel, h], far_r.at[q, rel, h])
            part[q][xx, k, rel, :, h * f:(h + 1) * f] = part[q][xx, k, rel, :, h * f:(h + 1) * f] + far_in[q][rel, h]
            send(part[q].at[xx, k, rel], near_in[q].at[rel, h],
                 near_s.at[q, rel, h], near_r.at[q, rel, h], at(dx=sgn))
        core_sum(q, rel, 0)

    def z_piece(q, dz):
        return back[q].at[pl.ds(((z + dz + 8) % 8) * CHUNKS[q], CHUNKS[q])]

    def z_half(q, dz, d):
        f = CHUNKS[q] // 2
        return back[q].at[pl.ds(((z + dz + 8) % 8) * 2 * f + d * f, f)]

    def z_start(q, rel):
        for h in range(2):
            got(near_in[q].at[rel, h], near_s.at[q, rel, h], near_r.at[q, rel, h])
        for i in range(3):
            v = part[q][x, k, rel, i] + near_in[q][rel, 0, i] + near_in[q][rel, 1, i]
            if rel == 0:
                back[q][pl.ds(z * CHUNKS[q], CHUNKS[q]), i * BLK:(i + 1) * BLK] = v
            else:
                other[q][:, i * BLK:(i + 1) * BLK] = v
        for d, sgn in ((0, 1), (1, -1)):
            if rel == 0:
                send(z_piece(q, 0), z_piece(q, 0), z_s.at[q, 2 + d], z_r.at[q, 2 + d], at(dz=2 * sgn))
            else:
                send(other[q], z_piece(q, 0), z_s.at[q, d], z_r.at[q, d], at(dz=sgn))

    def z_near(q):
        for d, sgn in ((0, 1), (1, -1)):
            ref = z_piece(q, -sgn)
            got(ref, z_s.at[q, d], z_r.at[q, d])
            send(ref, ref, z_s.at[q, 4 + d], z_r.at[q, 4 + d], at(dz=2 * sgn))

    def z_two(q):
        for d, sgn in ((0, 1), (1, -1)):
            got(z_piece(q, -2 * sgn), z_s.at[q, 2 + d], z_r.at[q, 2 + d])
            ref = z_half(q, -2 * sgn, d)
            send(ref, ref, z_s.at[q, 6 + d], z_r.at[q, 6 + d], at(dz=2 * sgn))

    def z_end(q):
        for d, sgn in ((0, 1), (1, -1)):
            got(z_piece(q, -3 * sgn), z_s.at[q, 4 + d], z_r.at[q, 4 + d])
        for d, sgn in ((0, 1), (1, -1)):
            got(z_half(q, -4 * sgn, d), z_s.at[q, 6 + d], z_r.at[q, 6 + d])

    def gw_dot(q):
        bh, bl = split(back[q][...])
        back_hi[q][...] = bh
        back_lo[q][...] = bl
        g = dot3(ft_hi[...], ft_lo[...], bh, bl, dot_nt)
        w = 2 * CHUNKS[q]
        for xx in range(4):
            v = g[:, xx * w:(xx + 1) * w].reshape(2, BLK, w)
            if w < BLK:
                v = jnp.concatenate([v[:, :64], v[:, 64:]], axis=2)
            gw[q][xx] = v
        gw_send(q)

    def gf(q):
        t = dot3(w_hi[q][...], w_lo[q][...], back_hi[q][...], back_lo[q][...], dot)
        if q > 0:
            t = gft[...] + t
        if q < Q - 1:
            gft[...] = t
        else:
            for i in range(3):
                for h in range(2):
                    gf_out[i * BLK:(i + 1) * BLK, h * BLK:(h + 1) * BLK] = (
                        t[h * BLK:(h + 1) * BLK, i * BLK:(i + 1) * BLK].T)

    def gw_row(q, j):
        rr = (r + j) % 8
        return copy(gw[q].at[rr // 2, rr % 2], gw_in[q].at[j], gwr_s.at[q, j], gwr_r.at[q, j],
                    {"row": rr, "col": c, "depth": zh})

    def gw_col(q, j):
        cc = (c + j) % 16
        return copy(gw_half[q].at[cc % (CHUNKS[q] // 4)], gw_yz[q].at[j], gwy_s.at[q, j], gwy_r.at[q, j],
                    {"row": r, "col": cc, "depth": zh})

    def gw_all(q, j):
        rr = (r + j) % 8
        return copy(gw_fin[q].at[r], gw_fin[q].at[r], gwf_s.at[q, j], gwf_r.at[q, j],
                    {"row": rr, "col": c, "depth": zh})

    def gw_all_in(q, j):
        ref = gw_fin[q].at[(r - j + 8) % 8]
        return copy(ref, ref, gwf_s.at[q, j], gwf_r.at[q, j], peer)

    def gw_send(q):
        @pl.loop(1, 8)
        def _(j):
            gw_row(q, j).start()

    def gw_sum(q):
        @pl.loop(1, 8)
        def _(j):
            gw_row(q, j).wait_recv()
        v = gw[q][x, k]
        for j in range(1, 8):
            v = v + gw_in[q][j]
        gw_half[q][...] = v.reshape(CHUNKS[q] // 4, 8, BLK)

        @pl.loop(1, 16)
        def _(j):
            gw_col(q, j).start()

    def gw_cols(q):
        @pl.loop(1, 16)
        def _(j):
            gw_col(q, j).wait_recv()
        v = gw_half[q][c % (CHUNKS[q] // 4)]
        for j in range(1, 16):
            v = v + gw_yz[q][j]
        if CHUNKS[q] == 32:
            v = jnp.concatenate([jnp.where(c < 8, v[:, :64], v[:, 64:])] * 2, axis=1)
        gw_fin[q][r] = v

        @pl.loop(1, 8)
        def _(j):
            gw_all(q, j).start()

    def gw_end():
        for q in range(Q):
            @pl.loop(1, 8)
            def _(j):
                gw_all_in(q, j).wait_recv()
        for zz in range(8):
            for kk in range(2):
                v = [gw_fin[q][(zz // 2) * 2 + kk][:, (zz % 2) * n:(zz % 2 + 1) * n] for q, n in enumerate(CHUNKS)]
                gw_out[kk * 8:(kk + 1) * 8, zz * BLK:(zz + 1) * BLK] = jnp.concatenate(v, axis=1)

    def drain():
        for cp in pending:
            cp.wait_send()
        blk_done()
        for q in range(Q):
            @pl.loop(1, 8)
            def _(j):
                gw_row(q, j).wait_send()
                gw_all(q, j).wait_send()

            @pl.loop(1, 16)
            def _(j):
                gw_col(q, j).wait_send()

    order = [
        (swap_send, 0), (swap_send, 1), (blk_send,), (y_first, 0, 0), (swap_wait, 0), (y_first, 0, 1),
        (y_step, 0, 1, 0), (prep_own,), (y_step, 0, 1, 1), (swap_wait, 1), (y_step, 0, 2, 0), (tab_make,),
        (y_step, 0, 2, 1), (prep_w,), (y_first, 1, 0), (y_step, 0, 3, 0), (y_step, 0, 3, 1), (y_first, 1, 1),
        (prep_feat,), (y_step, 1, 1, 0), (y_step, 0, 4, 1), (y_step, 0, 4, 0), (spmm, 0, 0), (y_step, 1, 1, 1),
        (core_send, 0, 0), (prep_peer,), (y_step, 1, 2, 0), (x_far, 0, 0), (spmm, 0, 1), (y_step, 1, 2, 1),
        (core_send, 0, 1), (x_near, 0, 0), (y_step, 1, 3, 0), (x_far, 0, 1), (y_step, 1, 3, 1), (z_start, 0, 0),
        (x_near, 0, 1), (y_step, 1, 4, 0), (y_step, 1, 4, 1), (spmm, 1, 0), (core_send, 1, 0), (z_start, 0, 1),
        (spmm, 1, 1), (core_send, 1, 1), (x_far, 1, 0), (z_near, 0), (x_far, 1, 1), (z_two, 0), (x_near, 1, 0),
        (x_near, 1, 1), (z_start, 1, 0), (z_start, 1, 1), (z_end, 0), (gw_dot, 0), (z_two, 1), (gf, 0),
        (z_near, 1), (gw_sum, 0), (z_end, 1), (gw_dot, 1), (gf, 1), (gw_cols, 0), (gw_sum, 1), (gw_cols, 1),
        (gw_end,), (drain,),
    ]
    for fn, *args in order:
        fn(*args)


def body(upstream, preact, features, weight, blocks, block_pos, block_count):
    vmem = pl.BlockSpec(memory_space=pltpu.VMEM)
    smem = pl.BlockSpec(memory_space=pltpu.SMEM)
    hbm = pl.BlockSpec(memory_space=pl.ANY)
    dma = pltpu.SemaphoreType.DMA
    V = pltpu.VMEM
    scratch = [
        V((2, 3, BLK, BLK), F32),
        V((8, BLK), jnp.int32), pltpu.SMEM((8, BLK), jnp.int32),
        V((8, BLK), jnp.int32), pltpu.SMEM((8, BLK), jnp.int32),
        V((32, BLK, BLK), F32), V((32, BLK, BLK), F32),
        V((2, 32, BLK, BLK), BF16), V((2, 32, BLK, BLK), BF16),
        V((32, max(CHUNKS), BLK), F32),
        V((384, 256), F32), V((256, 1024), F32),
        V((256, 384), BF16), V((256, 384), BF16),
        V((256, 384), F32),
    ]
    for shape, dtype in (
        (lambda f: (48, f, BLK), F32), (lambda f: (4, 2, 2, 3, f, BLK), F32), (lambda f: (4, 2, 3, f, BLK), F32),
        (lambda f: (2, 2, 3, f // 2, BLK), F32), (lambda f: (2, 2, 3, f, BLK), F32),
        (lambda f: (8 * f, 384), F32), (lambda f: (f, 384), F32),
        (lambda f: (8 * f, 384), BF16), (lambda f: (8 * f, 384), BF16),
        (lambda f: (256, 8 * f), BF16), (lambda f: (256, 8 * f), BF16),
        (lambda f: (4, 2, 2 * f, BLK), F32), (lambda f: (8, 2 * f, BLK), F32),
        (lambda f: (f // 4, 8, BLK), F32), (lambda f: (16, 8, BLK), F32), (lambda f: (8, 8, BLK), F32),
    ):
        scratch += [V(shape(f), dtype) for f in CHUNKS]
    scratch += [
        dma((5,)), dma((Q,)), dma((Q,)), dma((1,)), dma((1,)), dma((4,)), dma((4,)),
        dma((Q, 2, 2, 4)), dma((Q, 2, 2, 4)), dma((Q, 2, 4)), dma((Q, 2, 4)),
        dma((Q, 2, 2)), dma((Q, 2, 2)), dma((Q, 2, 2)), dma((Q, 2, 2)), dma((Q, 8)), dma((Q, 8)),
        dma((Q, 8)), dma((Q, 8)), dma((Q, 16)), dma((Q, 16)), dma((Q, 8)), dma((Q, 8)),
    ]
    return pl.pallas_call(
        kernel,
        out_shape=(jax.ShapeDtypeStruct((384, 256), F32), jax.ShapeDtypeStruct((16, 1024), F32)),
        in_specs=[vmem, vmem, vmem, smem, hbm, hbm, hbm],
        out_specs=(vmem, vmem),
        scratch_shapes=scratch,
        compiler_params=pltpu.CompilerParams(
            collective_id=0, has_side_effects=True, vmem_limit_bytes=56 * 2**20),
        cost_estimate=pl.CostEstimate(flops=2 * 10**9, bytes_accessed=6 * 2**20, transcendentals=0),
        name="graph_backward",
    )(upstream, preact, block_pos, block_count, features, weight, blocks.reshape(blocks.shape[2:]))


def solution(mesh):
    in_specs = (
        P(("row", "col"), "depth"),
        P(("row", "col"), "depth"),
        P(("col", "row"), "depth"),
        P("depth", None),
        P("row", "col", None, None, None),
        P("row", "col", None),
        P("row", "col"),
    )
    out_specs = (P(("col", "row"), "depth"), P(("depth", "col"), None))
    return jax.shard_map(body, mesh=mesh, in_specs=in_specs, out_specs=out_specs, check_vma=False)
```

```python
import jax
import jax.numpy as jnp
from jax import lax
from jax.experimental import pallas as pl
from jax.experimental.pallas import tpu as pltpu
from jax.sharding import PartitionSpec as P

BLK = 128
CHUNKS = (32, 32, 32, 32)
Q = len(CHUNKS)
START = tuple(sum(CHUNKS[:q]) for q in range(Q))
MESH = pl.DeviceIdType.MESH
F32 = jnp.float32
BF16 = jnp.bfloat16
NT = (((1,), (1,)), ((), ()))


def split(v):
    hi = v.astype(BF16)
    return hi, (v - hi.astype(F32)).astype(BF16)


def dot(a, b):
    return jnp.dot(a, b, preferred_element_type=F32)


def dot_nt(a, b):
    return lax.dot_general(a, b, NT, preferred_element_type=F32)


def dot3(ah, al, bh, bl, f):
    return f(ah, bh) + f(al, bh) + f(ah, bl)


def down(row):
    return jnp.broadcast_to(row, (BLK, BLK)).T


def tables(pos, count):
    lane = lax.broadcasted_iota(jnp.int32, (1, BLK), 1)
    ii = lax.broadcasted_iota(jnp.int32, (BLK, BLK), 0)
    jj = lax.broadcasted_iota(jnp.int32, (BLK, BLK), 1)
    live = (lane < count).astype(jnp.int32)
    brow = (pos * 2731) >> 16
    col = jnp.where(live > 0, pos - 24 * brow, 24)
    col_i = down(col)
    key = col * BLK + lane
    rank = jnp.sum((down(key) < key).astype(jnp.int32), axis=0, keepdims=True)
    same = (col_i == col).astype(jnp.int32)
    seen = jnp.sum(same * (ii < jj).astype(jnp.int32), axis=0, keepdims=True)
    more = jnp.sum(same * (ii > jj).astype(jnp.int32), axis=0, keepdims=True)
    cont = jnp.where(seen > 0, live, 0)
    rank_i = down(rank)
    hot = (rank_i == jj).astype(jnp.int32)

    def put(v):
        return jnp.sum(hot * v, axis=0, keepdims=True)

    at_col = (col_i == jj).astype(jnp.int32)
    last = jnp.sum(at_col * down(jnp.where(more > 0, 0, rank)), axis=0, keepdims=True)
    has = (jnp.sum(at_col, axis=0, keepdims=True) > 0).astype(jnp.int32)
    return [put(down(brow)), put(ii), put(down(live)), put(down(cont)), last, has]


def kernel(up_hbm, pre_hbm, pos, count, feat_hbm, w_hbm, blk_hbm, gf_hbm, gw_hbm,
           up, pre, gf_out, gw_out, turned, tab_v, tab_own, peer_tab_v, peer_tab, own_blk, peer_blk, blk_hi, blk_lo, run,
           feat, wv, ft_hi, ft_lo, gft, *rest):
    gwc, gwc_in, gwc_fin, *rest = rest
    parts = [rest[i * Q:(i + 1) * Q] for i in range(15)]
    (sig, part, core_in, near_in, back, other, back_hi, back_lo, w_hi, w_lo,
     gw, gw_in, gw_half, gw_yz, gw_fin) = parts
    (loc, swap_s, swap_r, tab_s, tab_r, blk_s, blk_r, y_s, y_r, core_s, core_r,
     near_s, near_r, z_s, z_r, gwr_s, gwr_r, gwy_s, gwy_r, gwf_s, gwf_r) = rest[15 * Q:]

    r = lax.axis_index("row")
    c = lax.axis_index("col")
    zh = lax.axis_index("depth")
    x, k = r // 2, r % 2
    y, zl = c // 2, c % 2
    z = zh * 2 + zl

    def at(dx=0, dk=0, dy=0, dz=0):
        zz = (z + dz + 8) % 8
        return {"row": ((x + dx + 4) % 4) * 2 + (k + dk) % 2,
                "col": ((y + dy + 8) % 8) * 2 + zz % 2, "depth": zz // 2}

    peer = {"row": r, "col": y * 2 + 1 - zl, "depth": zh}
    pending = []

    def copy(src, dst, ssem, rsem, dev):
        return pltpu.make_async_remote_copy(src_ref=src, dst_ref=dst, send_sem=ssem, recv_sem=rsem,
                                            device_id=dev, device_id_type=MESH)

    def send(src, dst, ssem, rsem, dev):
        cp = copy(src, dst, ssem, rsem, dev)
        cp.start()
        pending.append(cp)

    def got(dst, ssem, rsem):
        copy(dst, dst, ssem, rsem, peer).wait_recv()

    local = [pltpu.make_async_copy(s, d, loc.at[i]) for i, (s, d) in enumerate(
        ((blk_hbm, own_blk), (feat_hbm, feat), (w_hbm, wv), (up_hbm, up), (pre_hbm, pre)))]
    local[3].start()
    local[4].start()

    bar = pltpu.get_barrier_semaphore()
    for dev in (at(dx=2), at(dx=1), at(dx=-1), at(dk=1), at(dy=1), at(dy=-1), at(dz=1), at(dz=-1), at(dz=2), at(dz=-2)):
        pl.semaphore_signal(bar, inc=1, device_id=dev, device_id_type=MESH)

    local[3].wait()
    local[4].wait()

    for i in range(3):
        for h in range(2):
            u = up[i * BLK:(i + 1) * BLK, h * BLK:(h + 1) * BLK]
            p = pre[i * BLK:(i + 1) * BLK, h * BLK:(h + 1) * BLK]
            turned[h, i] = (u * (p > 0).astype(F32)).T
    for i in range(3):
        v = turned[zl, i]
        for q in range(Q):
            sig[q][6 * y + 3 * zl + i] = v[START[q]:START[q] + CHUNKS[q]]

    for cp in local[:3]:
        cp.start()

    pl.semaphore_wait(bar, 10)

    n_slots = jnp.where(r == 0, 32, 16)

    def swap_send(q):
        send(turned.at[1 - zl, :, pl.ds(START[q], CHUNKS[q])], sig[q].at[pl.ds(6 * y + 3 * zl, 3)],
             swap_s.at[q], swap_r.at[q], peer)

    def swap_wait(q):
        got(sig[q].at[pl.ds(6 * y + 3 * (1 - zl), 3)], swap_s.at[q], swap_r.at[q])

    def y_piece(q, yo, hr):
        h = zl if hr == 0 else 1 - zl
        return sig[q].at[pl.ds(6 * yo + 3 * h, 3)]

    def y_send(q, d, s, hr):
        sgn = 1 - 2 * d
        ref = y_piece(q, (y - sgn * (s - 1) + 8) % 8, hr)
        send(ref, ref, y_s.at[q, d, hr, s - 1], y_r.at[q, d, hr, s - 1], at(dy=sgn))

    def y_first(q, hr):
        for d in range(2):
            y_send(q, d, 1, hr)

    def y_step(q, s, hr):
        for d in range(2):
            last = 4 if d == hr else 3
            if s > last:
                continue
            sgn = 1 - 2 * d
            got(y_piece(q, (y - sgn * s + 8) % 8, hr), y_s.at[q, d, hr, s - 1], y_r.at[q, d, hr, s - 1])
            if s < last:
                y_send(q, d, s + 1, hr)

    def blk_copy(j):
        lo = 8 * j
        return copy(blk_hbm.at[pl.ds(lo, 8)], peer_blk.at[pl.ds(lo, 8)], blk_s.at[j], blk_r.at[j],
                    at(dz=1 if j % 2 == 0 else -1))

    def tab_make():
        tab_v[...] = jnp.zeros_like(tab_v)
        tab_v[0:1, 0:32] = pos[0]
        for i, v in enumerate(tables(tab_v[0:1], count[0, 0])):
            tab_v[i:i + 1] = v
        send(tab_v, peer_tab_v, tab_s.at[0], tab_r.at[0], peer)
        cp = pltpu.make_async_copy(tab_v, tab_own, loc.at[5])
        cp.start()
        cp.wait()

    def blk_send():
        for j in range(2):
            blk_copy(j).start()

        @pl.when(r == 0)
        def _():
            for j in range(2, 4):
                blk_copy(j).start()

    def blk_wait():
        for j in range(2):
            blk_copy(j).wait_recv()

        @pl.when(r == 0)
        def _():
            for j in range(2, 4):
                blk_copy(j).wait_recv()

    def blk_done():
        for j in range(2):
            blk_copy(j).wait_send()

        @pl.when(r == 0)
        def _():
            for j in range(2, 4):
                blk_copy(j).wait_send()

    def split_blocks(rel):
        src = own_blk if rel == 0 else peer_blk

        @pl.loop(0, n_slots)
        def _(i):
            hi, lo = split(src[i])
            blk_hi[rel, i] = hi
            blk_lo[rel, i] = lo

    def prep_own():
        local[0].wait()
        split_blocks(0)

    def prep_peer():
        got(peer_tab_v, tab_s.at[0], tab_r.at[0])
        cp = pltpu.make_async_copy(peer_tab_v, peer_tab, loc.at[3])
        cp.start()
        blk_wait()
        split_blocks(1)
        cp.wait()

    def prep_feat():
        local[1].wait()
        for i in range(3):
            for h in range(2):
                t = feat[i * BLK:(i + 1) * BLK, h * BLK:(h + 1) * BLK].T
                t = t.reshape(8, 2, 8, BLK)
                for kk in range(2):
                    hi, lo = split(t[:, kk].reshape(64, BLK))
                    row = kk * BLK + h * 64
                    ft_hi[row:row + 64, i * BLK:(i + 1) * BLK] = hi
                    ft_lo[row:row + 64, i * BLK:(i + 1) * BLK] = lo

    def prep_w():
        local[2].wait()
        for q in range(Q):
            lo, n = START[q], CHUNKS[q]
            v = jnp.concatenate([wv[:, zz * BLK + lo:zz * BLK + lo + n] for zz in range(8)], axis=1)
            w_hi[q][...], w_lo[q][...] = split(v)

    def spmm(q, rel):
        tab = tab_own if rel == 0 else peer_tab
        f = CHUNKS[q]

        def step(it, acc):
            terms = []
            for u in range(4):
                i = it * 4 + u
                sh, sl = split(sig[q][tab[0, i]])
                o = tab[1, i]
                t = dot(jnp.concatenate([sh, sl], axis=0), blk_hi[rel, o])
                t = t[:f] + t[f:] + dot(sh, blk_lo[rel, o])
                terms.append(t * tab[2, i].astype(F32))
            for u in range(4):
                i = it * 4 + u
                acc = terms[u] + acc * tab[3, i].astype(F32)
                run[i, 0:f] = acc
            return acc

        lax.fori_loop(0, n_slots // 4, step, jnp.zeros((f, BLK), F32))
        for b in range(24):
            rr = b // 3
            part[q][rr // 2, rr % 2, rel, b % 3] = run[tab[4, b], 0:f] * tab[5, b].astype(F32)

    def core_send(q, rel):
        for o in (2, 1, 3, 0):
            xx = (x + o) % 4
            send(part[q].at[xx, 1 - k, rel], core_in[q].at[xx, rel],
                 core_s.at[q, rel, o], core_r.at[q, rel, o], at(dk=1))

    def core_sum(q, rel, o):
        xx = (x + o) % 4
        got(core_in[q].at[xx, rel], core_s.at[q, rel, o], core_r.at[q, rel, o])
        part[q][xx, k, rel] = part[q][xx, k, rel] + core_in[q][xx, rel]

    def x_send(q, rel, o):
        core_sum(q, rel, o)
        send(part[q].at[(x + o) % 4, k, rel], near_in[q].at[rel, o - 1],
             near_s.at[q, rel, o - 1], near_r.at[q, rel, o - 1], at(dx=o))

    def x_far(q, rel):
        x_send(q, rel, 2)

    def x_near(q, rel):
        x_send(q, rel, 1)
        x_send(q, rel, 3)
        core_sum(q, rel, 0)

    def z_piece(q, dz):
        return back[q].at[pl.ds(((z + dz + 8) % 8) * CHUNKS[q], CHUNKS[q])]

    def z_half(q, dz, d):
        f = CHUNKS[q] // 2
        return back[q].at[pl.ds(((z + dz + 8) % 8) * 2 * f + d * f, f)]

    def z_start(q, rel):
        for h in range(3):
            got(near_in[q].at[rel, h], near_s.at[q, rel, h], near_r.at[q, rel, h])
        for i in range(3):
            v = (part[q][x, k, rel, i] + near_in[q][rel, 0, i]) + (near_in[q][rel, 1, i] + near_in[q][rel, 2, i])
            if rel == 0:
                back[q][pl.ds(z * CHUNKS[q], CHUNKS[q]), i * BLK:(i + 1) * BLK] = v
            else:
                other[q][:, i * BLK:(i + 1) * BLK] = v
        for d, sgn in ((0, 1), (1, -1)):
            if rel == 0:
                send(z_piece(q, 0), z_piece(q, 0), z_s.at[q, 2 + d], z_r.at[q, 2 + d], at(dz=2 * sgn))
            else:
                send(other[q], z_piece(q, 0), z_s.at[q, d], z_r.at[q, d], at(dz=sgn))

    def z_near(q):
        for d, sgn in ((0, 1), (1, -1)):
            ref = z_piece(q, -sgn)
            got(ref, z_s.at[q, d], z_r.at[q, d])
            send(ref, ref, z_s.at[q, 4 + d], z_r.at[q, 4 + d], at(dz=2 * sgn))

    def z_two(q):
        for d, sgn in ((0, 1), (1, -1)):
            got(z_piece(q, -2 * sgn), z_s.at[q, 2 + d], z_r.at[q, 2 + d])
            ref = z_half(q, -2 * sgn, d)
            send(ref, ref, z_s.at[q, 6 + d], z_r.at[q, 6 + d], at(dz=2 * sgn))

    def z_end(q):
        for d, sgn in ((0, 1), (1, -1)):
            got(z_piece(q, -3 * sgn), z_s.at[q, 4 + d], z_r.at[q, 4 + d])
        for d, sgn in ((0, 1), (1, -1)):
            got(z_half(q, -4 * sgn, d), z_s.at[q, 6 + d], z_r.at[q, 6 + d])

    def gw_dot(q):
        bh, bl = split(back[q][...])
        back_hi[q][...] = bh
        back_lo[q][...] = bl
        g = dot3(ft_hi[...], ft_lo[...], bh, bl, dot_nt)
        if q == Q - 1:
            for kk in range(2):
                gwc[:, kk] = g[kk * BLK:(kk + 1) * BLK].reshape(16, 8, 8 * CHUNKS[q])

            @pl.loop(0, 15)
            def _(i):
                gwc_col(far16(i)).start()
            return
        w = 2 * CHUNKS[q]
        for xx in range(4):
            v = g[:, xx * w:(xx + 1) * w].reshape(2, BLK, w)
            if w < BLK:
                v = jnp.concatenate([v[:, :64], v[:, 64:]], axis=2)
            gw[q][xx] = v
        gw_send(q)

    def gf(q):
        t = dot3(w_hi[q][...], w_lo[q][...], back_hi[q][...], back_lo[q][...], dot)
        if q > 0:
            t = gft[...] + t
        if q < Q - 1:
            gft[...] = t
        else:
            for i in range(3):
                for h in range(2):
                    gf_out[i * BLK:(i + 1) * BLK, h * BLK:(h + 1) * BLK] = (
                        t[h * BLK:(h + 1) * BLK, i * BLK:(i + 1) * BLK].T)
            pltpu.make_async_copy(gf_out, gf_hbm, loc.at[7]).start()

    def far8(i):
        return 4 + (1 - 2 * (i % 2)) * ((i + 1) // 2)

    def far16(i):
        return 8 + (1 - 2 * (i % 2)) * ((i + 1) // 2)

    def gw_row(q, j):
        rr = (r + j) % 8
        return copy(gw[q].at[rr // 2, rr % 2], gw_in[q].at[j], gwr_s.at[q, j], gwr_r.at[q, j],
                    {"row": rr, "col": c, "depth": zh})

    def gw_col(q, j):
        cc = (c + j) % 16
        return copy(gw_half[q].at[cc % (CHUNKS[q] // 4)], gw_yz[q].at[j], gwy_s.at[q, j], gwy_r.at[q, j],
                    {"row": r, "col": cc, "depth": zh})

    def gw_all(q, j):
        rr = (r + j) % 8
        ref = (gwc_fin if q == Q - 1 else gw_fin[q]).at[r]
        return copy(ref, ref, gwf_s.at[q, j], gwf_r.at[q, j], {"row": rr, "col": c, "depth": zh})

    def gw_all_in(q, j):
        ref = (gwc_fin if q == Q - 1 else gw_fin[q]).at[(r - j + 8) % 8]
        return copy(ref, ref, gwf_s.at[q, j], gwf_r.at[q, j], peer)

    def gwc_col(j):
        cc = (c + j) % 16
        return copy(gwc.at[cc], gwc_in.at[j], gwy_s.at[Q - 1, j], gwy_r.at[Q - 1, j],
                    {"row": r, "col": cc, "depth": zh})

    def gw_send(q):
        @pl.loop(0, 7)
        def _(i):
            gw_row(q, far8(i)).start()

    def gw_sum(q):
        @pl.loop(1, 8)
        def _(j):
            gw_row(q, j).wait_recv()
        v = gw[q][x, k]
        for j in range(1, 8):
            v = v + gw_in[q][j]
        gw_half[q][...] = v.reshape(CHUNKS[q] // 4, 8, BLK)

        @pl.loop(0, 15)
        def _(i):
            gw_col(q, far16(i)).start()

    def gw_cols(q):
        if q == Q - 1:
            @pl.loop(1, 16)
            def _(j):
                gwc_col(j).wait_recv()
            v = gwc[c]
            for j in range(1, 16):
                v = v + gwc_in[j]
            gwc_fin[r] = v
        else:
            @pl.loop(1, 16)
            def _(j):
                gw_col(q, j).wait_recv()
            v = gw_half[q][c % (CHUNKS[q] // 4)]
            for j in range(1, 16):
                v = v + gw_yz[q][j]
            if CHUNKS[q] == 32:
                v = jnp.concatenate([jnp.where(c < 8, v[:, :64], v[:, 64:])] * 2, axis=1)
            gw_fin[q][r] = v

        @pl.loop(0, 7)
        def _(i):
            gw_all(q, far8(i)).start()

    def gw_end(q):
        @pl.loop(1, 8)
        def _(j):
            gw_all_in(q, j).wait_recv()
        n = CHUNKS[q]
        for kk in range(2):
            if q == Q - 1:
                v = gwc_fin[0, kk]
                for j in range(1, 8):
                    v = v + gwc_fin[j, kk]
            for zz in range(8):
                if q == Q - 1:
                    u = v[:, zz * n:(zz + 1) * n]
                else:
                    u = gw_fin[q][(zz // 2) * 2 + kk][:, (zz % 2) * n:(zz % 2 + 1) * n]
                lane = zz * BLK + START[q]
                gw_out[kk * 8:(kk + 1) * 8, lane:lane + n] = u

    def early():
        for cp in pending:
            cp.wait_send()
        pending.clear()
        blk_done()
        for q in range(Q - 1):
            @pl.loop(1, 8)
            def _(j):
                gw_row(q, j).wait_send()

    def drain():
        last = pltpu.make_async_copy(gw_out, gw_hbm, loc.at[8])
        last.start()
        for cp in pending:
            cp.wait_send()
        for q in range(Q):
            @pl.loop(1, 8)
            def _(j):
                gw_all(q, j).wait_send()

            @pl.loop(1, 16)
            def _(j):
                (gwc_col(j) if q == Q - 1 else gw_col(q, j)).wait_send()
        pltpu.make_async_copy(gf_out, gf_hbm, loc.at[7]).wait()
        last.wait()

    order = [
        (swap_send, 0), (swap_send, 1), (y_first, 0, 0), (swap_send, 2), (blk_send,), (prep_feat,), (prep_w,),
        (swap_wait, 0), (y_first, 0, 1), (y_step, 0, 1, 0), (y_first, 1, 0), (swap_wait, 1), (swap_send, 3),
        (y_first, 1, 1), (tab_make,), (swap_wait, 2), (prep_own,), (y_step, 0, 1, 1), (y_step, 0, 2, 0),
        (y_step, 1, 1, 0), (y_step, 0, 2, 1), (y_step, 1, 1, 1), (y_first, 2, 0), (y_step, 0, 3, 0),
        (y_step, 0, 3, 1), (y_step, 1, 2, 0), (y_first, 2, 1), (y_step, 1, 2, 1), (y_step, 2, 1, 0),
        (y_step, 0, 4, 0), (y_step, 0, 4, 1), (spmm, 0, 0), (y_step, 1, 3, 0), (core_send, 0, 0),
        (y_step, 2, 1, 1), (y_step, 1, 3, 1), (y_first, 3, 0), (x_far, 0, 0), (y_step, 2, 2, 0), (prep_peer,),
        (spmm, 0, 1), (swap_wait, 3), (y_step, 2, 2, 1), (y_first, 3, 1), (core_send, 0, 1), (y_step, 1, 4, 1),
        (x_near, 0, 0), (y_step, 1, 4, 0), (spmm, 1, 0), (y_step, 3, 1, 0), (x_far, 0, 1), (core_send, 1, 0),
        (y_step, 2, 3, 1), (y_step, 2, 3, 0), (x_near, 0, 1), (y_step, 3, 1, 1), (z_start, 0, 0), (spmm, 1, 1),
        (x_far, 1, 0), (y_step, 3, 2, 0), (x_near, 1, 0), (core_send, 1, 1), (z_start, 0, 1), (y_step, 2, 4, 0),
        (y_step, 3, 2, 1), (y_step, 2, 4, 1), (spmm, 2, 0), (x_far, 1, 1), (y_step, 3, 3, 0), (x_near, 1, 1),
        (z_start, 1, 0), (core_send, 2, 0), (z_near, 0), (y_step, 3, 3, 1), (spmm, 2, 1), (x_far, 2, 0),
        (y_step, 3, 4, 0), (z_two, 0), (core_send, 2, 1), (x_near, 2, 0), (z_start, 1, 1), (y_step, 3, 4, 1),
        (spmm, 3, 0), (core_send, 3, 0), (z_two, 1), (x_far, 2, 1), (x_near, 2, 1), (z_start, 2, 0),
        (spmm, 3, 1), (x_far, 3, 0), (core_send, 3, 1), (z_near, 1), (x_near, 3, 0), (x_far, 3, 1),
        (z_start, 2, 1), (z_end, 0), (x_near, 3, 1), (z_two, 2), (z_start, 3, 0), (gw_dot, 0), (z_start, 3, 1),
        (z_end, 1), (z_near, 2), (gw_dot, 1), (z_two, 3), (gf, 0), (z_near, 3), (gf, 1), (gw_sum, 0),
        (z_end, 2), (gw_dot, 2), (gw_sum, 1), (z_end, 3), (gw_dot, 3), (gf, 2), (early,), (gf, 3), (gw_sum, 2),
        (gw_cols, 1), (gw_cols, 0), (gw_end, 1), (gw_cols, 3), (gw_cols, 2), (gw_end, 0), (gw_end, 3),
        (gw_end, 2), (drain,),
    ]
    for fn, *args in order:
        fn(*args)


def body(upstream, preact, features, weight, blocks, block_pos, block_count):
    vmem = pl.BlockSpec(memory_space=pltpu.VMEM)
    smem = pl.BlockSpec(memory_space=pltpu.SMEM)
    hbm = pl.BlockSpec(memory_space=pl.ANY)
    dma = pltpu.SemaphoreType.DMA
    V = pltpu.VMEM
    scratch = [
        V((384, 256), F32), V((384, 256), F32),
        V((384, 256), F32), V((16, 1024), F32),
        V((2, 3, BLK, BLK), F32),
        V((8, BLK), jnp.int32), pltpu.SMEM((8, BLK), jnp.int32),
        V((8, BLK), jnp.int32), pltpu.SMEM((8, BLK), jnp.int32),
        V((32, BLK, BLK), F32), V((32, BLK, BLK), F32),
        V((2, 32, BLK, BLK), BF16), V((2, 32, BLK, BLK), BF16),
        V((32, max(CHUNKS), BLK), F32),
        V((384, 256), F32), V((256, 1024), F32),
        V((256, 384), BF16), V((256, 384), BF16),
        V((256, 384), F32),
        V((16, 2, 8, 8 * CHUNKS[-1]), F32), V((16, 2, 8, 8 * CHUNKS[-1]), F32), V((8, 2, 8, 8 * CHUNKS[-1]), F32),
    ]
    for shape, dtype in (
        (lambda f: (48, f, BLK), F32), (lambda f: (4, 2, 2, 3, f, BLK), F32), (lambda f: (4, 2, 3, f, BLK), F32),
        (lambda f: (2, 3, 3, f, BLK), F32),
        (lambda f: (8 * f, 384), F32), (lambda f: (f, 384), F32),
        (lambda f: (8 * f, 384), BF16), (lambda f: (8 * f, 384), BF16),
        (lambda f: (256, 8 * f), BF16), (lambda f: (256, 8 * f), BF16),
        (lambda f: (4, 2, 2 * f, BLK), F32), (lambda f: (8, 2 * f, BLK), F32),
        (lambda f: (f // 4, 8, BLK), F32), (lambda f: (16, 8, BLK), F32), (lambda f: (8, 8, BLK), F32),
    ):
        scratch += [V(shape(f), dtype) for f in CHUNKS]
    scratch += [
        dma((9,)), dma((Q,)), dma((Q,)), dma((1,)), dma((1,)), dma((4,)), dma((4,)),
        dma((Q, 2, 2, 4)), dma((Q, 2, 2, 4)), dma((Q, 2, 4)), dma((Q, 2, 4)),
        dma((Q, 2, 3)), dma((Q, 2, 3)), dma((Q, 8)), dma((Q, 8)),
        dma((Q, 8)), dma((Q, 8)), dma((Q, 16)), dma((Q, 16)), dma((Q, 8)), dma((Q, 8)),
    ]
    return pl.pallas_call(
        kernel,
        out_shape=(jax.ShapeDtypeStruct((384, 256), F32), jax.ShapeDtypeStruct((16, 1024), F32)),
        in_specs=[hbm, hbm, vmem, smem, hbm, hbm, hbm],
        out_specs=(hbm, hbm),
        scratch_shapes=scratch,
        compiler_params=pltpu.CompilerParams(
            collective_id=0, has_side_effects=True, vmem_limit_bytes=56 * 2**20),
        cost_estimate=pl.CostEstimate(flops=2 * 10**9, bytes_accessed=6 * 2**20, transcendentals=0),
        name="graph_backward",
    )(upstream, preact, block_pos, block_count, features, weight, blocks.reshape(blocks.shape[2:]))


def solution(mesh):
    in_specs = (
        P(("row", "col"), "depth"),
        P(("row", "col"), "depth"),
        P(("col", "row"), "depth"),
        P("depth", None),
        P("row", "col", None, None, None),
        P("row", "col", None),
        P("row", "col"),
    )
    out_specs = (P(("col", "row"), "depth"), P(("depth", "col"), None))
    return jax.shard_map(body, mesh=mesh, in_specs=in_specs, out_specs=out_specs, check_vma=False)
```

```python
import jax
import jax.numpy as jnp
from jax import lax
from jax.experimental import pallas as pl
from jax.experimental.pallas import tpu as pltpu
from jax.sharding import PartitionSpec as P

BLK = 128
CHUNKS = (32, 32, 32, 32)
Q = len(CHUNKS)
START = tuple(sum(CHUNKS[:q]) for q in range(Q))
MESH = pl.DeviceIdType.MESH
F32 = jnp.float32
BF16 = jnp.bfloat16
NT = (((1,), (1,)), ((), ()))


def split(v):
    hi = v.astype(BF16)
    return hi, (v - hi.astype(F32)).astype(BF16)


def dot(a, b):
    return jnp.dot(a, b, preferred_element_type=F32)


def dot_nt(a, b):
    return lax.dot_general(a, b, NT, preferred_element_type=F32)


def dot3(ah, al, bh, bl, f):
    return f(ah, bh) + f(al, bh) + f(ah, bl)


def down(row):
    return jnp.broadcast_to(row, (BLK, BLK)).T


def tables(pos, count):
    lane = lax.broadcasted_iota(jnp.int32, (1, BLK), 1)
    ii = lax.broadcasted_iota(jnp.int32, (BLK, BLK), 0)
    jj = lax.broadcasted_iota(jnp.int32, (BLK, BLK), 1)
    live = (lane < count).astype(jnp.int32)
    brow = (pos * 2731) >> 16
    col = jnp.where(live > 0, pos - 24 * brow, 24)
    col_i = down(col)
    key = col * BLK + lane
    rank = jnp.sum((down(key) < key).astype(jnp.int32), axis=0, keepdims=True)
    same = (col_i == col).astype(jnp.int32)
    seen = jnp.sum(same * (ii < jj).astype(jnp.int32), axis=0, keepdims=True)
    more = jnp.sum(same * (ii > jj).astype(jnp.int32), axis=0, keepdims=True)
    cont = jnp.where(seen > 0, live, 0)
    rank_i = down(rank)
    hot = (rank_i == jj).astype(jnp.int32)

    def put(v):
        return jnp.sum(hot * v, axis=0, keepdims=True)

    at_col = (col_i == jj).astype(jnp.int32)
    last = jnp.sum(at_col * down(jnp.where(more > 0, 0, rank)), axis=0, keepdims=True)
    has = (jnp.sum(at_col, axis=0, keepdims=True) > 0).astype(jnp.int32)
    return [put(down(brow)), put(ii), put(down(live)), put(down(cont)), last, has]


def kernel(up_hbm, pre_hbm, pos, count, feat_hbm, w_hbm, blk_hbm, gf_hbm, gw_hbm,
           up, pre, gf_out, gw_out, turned, tab_v, tab_own, peer_tab_v, peer_tab, own_blk, peer_blk, blk_hi, blk_lo, run,
           feat, wv, ft_hi, ft_lo, gft, *rest):
    gwc, gwc_in, gwc_fin, gw_half, gw_yz, gw_fin, *rest = rest
    parts = [rest[i * Q:(i + 1) * Q] for i in range(12)]
    (sig, part, core_in, near_in, back, other, back_hi, back_lo, w_hi, w_lo,
     gw, gw_in) = parts
    (loc, swap_s, swap_r, tab_s, tab_r, blk_s, blk_r, y_s, y_r, core_s, core_r,
     near_s, near_r, z_s, z_r, gwr_s, gwr_r, gwy_s, gwy_r, gwf_s, gwf_r) = rest[12 * Q:]

    r = lax.axis_index("row")
    c = lax.axis_index("col")
    zh = lax.axis_index("depth")
    x, k = r // 2, r % 2
    y, zl = c // 2, c % 2
    z = zh * 2 + zl

    def at(dx=0, dk=0, dy=0, dz=0):
        zz = (z + dz + 8) % 8
        return {"row": ((x + dx + 4) % 4) * 2 + (k + dk) % 2,
                "col": ((y + dy + 8) % 8) * 2 + zz % 2, "depth": zz // 2}

    peer = {"row": r, "col": y * 2 + 1 - zl, "depth": zh}
    pending = []

    def copy(src, dst, ssem, rsem, dev):
        return pltpu.make_async_remote_copy(src_ref=src, dst_ref=dst, send_sem=ssem, recv_sem=rsem,
                                            device_id=dev, device_id_type=MESH)

    def send(src, dst, ssem, rsem, dev):
        cp = copy(src, dst, ssem, rsem, dev)
        cp.start()
        pending.append(cp)

    def got(dst, ssem, rsem):
        copy(dst, dst, ssem, rsem, peer).wait_recv()

    local = [pltpu.make_async_copy(s, d, loc.at[i]) for i, (s, d) in enumerate(
        ((blk_hbm, own_blk), (feat_hbm, feat), (w_hbm, wv), (up_hbm, up), (pre_hbm, pre)))]
    local[3].start()
    local[4].start()

    bar = pltpu.get_barrier_semaphore()
    for dev in (at(dx=2), at(dx=1), at(dx=-1), at(dk=1), at(dy=1), at(dy=-1), at(dz=1), at(dz=-1), at(dz=2), at(dz=-2)):
        pl.semaphore_signal(bar, inc=1, device_id=dev, device_id_type=MESH)

    local[3].wait()
    local[4].wait()

    for i in range(3):
        for h in range(2):
            u = up[i * BLK:(i + 1) * BLK, h * BLK:(h + 1) * BLK]
            p = pre[i * BLK:(i + 1) * BLK, h * BLK:(h + 1) * BLK]
            turned[h, i] = (u * (p > 0).astype(F32)).T
    for i in range(3):
        v = turned[zl, i]
        for q in range(Q):
            sig[q][6 * y + 3 * zl + i] = v[START[q]:START[q] + CHUNKS[q]]

    for cp in local[:3]:
        cp.start()

    pl.semaphore_wait(bar, 10)

    n_slots = jnp.where(r == 0, 32, 16)

    def swap_send(q):
        send(turned.at[1 - zl, :, pl.ds(START[q], CHUNKS[q])], sig[q].at[pl.ds(6 * y + 3 * zl, 3)],
             swap_s.at[q], swap_r.at[q], peer)

    def swap_wait(q):
        got(sig[q].at[pl.ds(6 * y + 3 * (1 - zl), 3)], swap_s.at[q], swap_r.at[q])

    def y_piece(q, yo, hr):
        h = zl if hr == 0 else 1 - zl
        return sig[q].at[pl.ds(6 * yo + 3 * h, 3)]

    def y_send(q, d, s, hr):
        sgn = 1 - 2 * d
        ref = y_piece(q, (y - sgn * (s - 1) + 8) % 8, hr)
        send(ref, ref, y_s.at[q, d, hr, s - 1], y_r.at[q, d, hr, s - 1], at(dy=sgn))

    def y_first(q, hr):
        for d in range(2):
            y_send(q, d, 1, hr)

    def y_step(q, s, hr):
        for d in range(2):
            last = 4 if d == hr else 3
            if s > last:
                continue
            sgn = 1 - 2 * d
            got(y_piece(q, (y - sgn * s + 8) % 8, hr), y_s.at[q, d, hr, s - 1], y_r.at[q, d, hr, s - 1])
            if s < last:
                y_send(q, d, s + 1, hr)

    def blk_copy(j):
        lo = 8 * j
        return copy(blk_hbm.at[pl.ds(lo, 8)], peer_blk.at[pl.ds(lo, 8)], blk_s.at[j], blk_r.at[j],
                    at(dz=1 if j % 2 == 0 else -1))

    def tab_make():
        tab_v[...] = jnp.zeros_like(tab_v)
        tab_v[0:1, 0:32] = pos[0]
        for i, v in enumerate(tables(tab_v[0:1], count[0, 0])):
            tab_v[i:i + 1] = v
        send(tab_v, peer_tab_v, tab_s.at[0], tab_r.at[0], peer)
        cp = pltpu.make_async_copy(tab_v, tab_own, loc.at[5])
        cp.start()
        cp.wait()

    def blk_send():
        for j in range(2):
            blk_copy(j).start()

        @pl.when(r == 0)
        def _():
            for j in range(2, 4):
                blk_copy(j).start()

    def blk_wait():
        for j in range(2):
            blk_copy(j).wait_recv()

        @pl.when(r == 0)
        def _():
            for j in range(2, 4):
                blk_copy(j).wait_recv()

    def blk_done():
        for j in range(2):
            blk_copy(j).wait_send()

        @pl.when(r == 0)
        def _():
            for j in range(2, 4):
                blk_copy(j).wait_send()

    def split_blocks(rel):
        src = own_blk if rel == 0 else peer_blk

        @pl.loop(0, n_slots)
        def _(i):
            hi, lo = split(src[i])
            blk_hi[rel, i] = hi
            blk_lo[rel, i] = lo

    def prep_own():
        local[0].wait()
        split_blocks(0)

    def prep_peer():
        got(peer_tab_v, tab_s.at[0], tab_r.at[0])
        cp = pltpu.make_async_copy(peer_tab_v, peer_tab, loc.at[3])
        cp.start()
        blk_wait()
        split_blocks(1)
        cp.wait()

    def prep_feat():
        local[1].wait()
        for i in range(3):
            for h in range(2):
                t = feat[i * BLK:(i + 1) * BLK, h * BLK:(h + 1) * BLK].T
                t = t.reshape(8, 2, 8, BLK)
                for kk in range(2):
                    hi, lo = split(t[:, kk].reshape(64, BLK))
                    row = kk * BLK + h * 64
                    ft_hi[row:row + 64, i * BLK:(i + 1) * BLK] = hi
                    ft_lo[row:row + 64, i * BLK:(i + 1) * BLK] = lo

    def prep_w():
        local[2].wait()
        for q in range(Q):
            lo, n = START[q], CHUNKS[q]
            v = jnp.concatenate([wv[:, zz * BLK + lo:zz * BLK + lo + n] for zz in range(8)], axis=1)
            w_hi[q][...], w_lo[q][...] = split(v)

    def spmm(q, rel):
        tab = tab_own if rel == 0 else peer_tab
        f = CHUNKS[q]

        def step(it, acc):
            terms = []
            for u in range(4):
                i = it * 4 + u
                sh, sl = split(sig[q][tab[0, i]])
                o = tab[1, i]
                t = dot(jnp.concatenate([sh, sl], axis=0), blk_hi[rel, o])
                t = t[:f] + t[f:] + dot(sh, blk_lo[rel, o])
                terms.append(t * tab[2, i].astype(F32))
            for u in range(4):
                i = it * 4 + u
                acc = terms[u] + acc * tab[3, i].astype(F32)
                run[i, 0:f] = acc
            return acc

        lax.fori_loop(0, n_slots // 4, step, jnp.zeros((f, BLK), F32))
        for b in range(24):
            rr = b // 3
            part[q][rr // 2, rr % 2, rel, b % 3] = run[tab[4, b], 0:f] * tab[5, b].astype(F32)

    def core_send(q, rel):
        for o in (2, 1, 3, 0):
            xx = (x + o) % 4
            send(part[q].at[xx, 1 - k, rel], core_in[q].at[xx, rel],
                 core_s.at[q, rel, o], core_r.at[q, rel, o], at(dk=1))

    def core_sum(q, rel, o):
        xx = (x + o) % 4
        got(core_in[q].at[xx, rel], core_s.at[q, rel, o], core_r.at[q, rel, o])
        part[q][xx, k, rel] = part[q][xx, k, rel] + core_in[q][xx, rel]

    def x_send(q, rel, o):
        core_sum(q, rel, o)
        send(part[q].at[(x + o) % 4, k, rel], near_in[q].at[rel, o - 1],
             near_s.at[q, rel, o - 1], near_r.at[q, rel, o - 1], at(dx=o))

    def x_far(q, rel):
        x_send(q, rel, 2)

    def x_near(q, rel):
        x_send(q, rel, 1)
        x_send(q, rel, 3)
        core_sum(q, rel, 0)

    def z_piece(q, dz):
        return back[q].at[pl.ds(((z + dz + 8) % 8) * CHUNKS[q], CHUNKS[q])]

    def z_half(q, dz, d):
        f = CHUNKS[q] // 2
        return back[q].at[pl.ds(((z + dz + 8) % 8) * 2 * f + d * f, f)]

    def z_start(q, rel):
        for h in range(3):
            got(near_in[q].at[rel, h], near_s.at[q, rel, h], near_r.at[q, rel, h])
        for i in range(3):
            v = (part[q][x, k, rel, i] + near_in[q][rel, 0, i]) + (near_in[q][rel, 1, i] + near_in[q][rel, 2, i])
            if rel == 0:
                back[q][pl.ds(z * CHUNKS[q], CHUNKS[q]), i * BLK:(i + 1) * BLK] = v
            else:
                other[q][:, i * BLK:(i + 1) * BLK] = v
        for d, sgn in ((0, 1), (1, -1)):
            if rel == 0:
                send(z_piece(q, 0), z_piece(q, 0), z_s.at[q, 2 + d], z_r.at[q, 2 + d], at(dz=2 * sgn))
            else:
                send(other[q], z_piece(q, 0), z_s.at[q, d], z_r.at[q, d], at(dz=sgn))

    def z_near(q):
        for d, sgn in ((0, 1), (1, -1)):
            ref = z_piece(q, -sgn)
            got(ref, z_s.at[q, d], z_r.at[q, d])
            send(ref, ref, z_s.at[q, 4 + d], z_r.at[q, 4 + d], at(dz=2 * sgn))

    def z_two(q):
        for d, sgn in ((0, 1), (1, -1)):
            got(z_piece(q, -2 * sgn), z_s.at[q, 2 + d], z_r.at[q, 2 + d])
            ref = z_half(q, -2 * sgn, d)
            send(ref, ref, z_s.at[q, 6 + d], z_r.at[q, 6 + d], at(dz=2 * sgn))

    def z_end(q):
        for d, sgn in ((0, 1), (1, -1)):
            got(z_piece(q, -3 * sgn), z_s.at[q, 4 + d], z_r.at[q, 4 + d])
        for d, sgn in ((0, 1), (1, -1)):
            got(z_half(q, -4 * sgn, d), z_s.at[q, 6 + d], z_r.at[q, 6 + d])

    def gw_dot(q):
        bh, bl = split(back[q][...])
        back_hi[q][...] = bh
        back_lo[q][...] = bl
        g = dot3(ft_hi[...], ft_lo[...], bh, bl, dot_nt)
        if q == Q - 1:
            for kk in range(2):
                gwc[:, kk] = g[kk * BLK:(kk + 1) * BLK].reshape(16, 8, 8 * CHUNKS[q])

            for i in range(15):
                gw_col(1, far16(i)).start()
            return
        w = 2 * CHUNKS[q]
        for xx in range(4):
            v = g[:, xx * w:(xx + 1) * w].reshape(2, BLK, w)
            if w < BLK:
                v = jnp.concatenate([v[:, :64], v[:, 64:]], axis=2)
            gw[q][xx] = v
        gw_send(q)

    def gf(q):
        t = dot3(w_hi[q][...], w_lo[q][...], back_hi[q][...], back_lo[q][...], dot)
        if q > 0:
            t = gft[...] + t
        if q < Q - 1:
            gft[...] = t
        else:
            gf_out[...] = t
            pltpu.make_async_copy(gf_out, gf_hbm, loc.at[7]).start()

    def far8(i):
        return 4 + (1 - 2 * (i % 2)) * ((i + 1) // 2)

    def far16(i):
        return 8 + (1 - 2 * (i % 2)) * ((i + 1) // 2)

    def gw_row(q, j):
        rr = (r + j) % 8
        return copy(gw[q].at[rr // 2, rr % 2], gw_in[q].at[j], gwr_s.at[q], gwr_r.at[q],
                    {"row": rr, "col": c, "depth": zh})

    def gw_rows(q):
        ref = gw_in[q].at[pl.ds(1, 7)]
        return copy(ref, ref, gwr_s.at[q], gwr_r.at[q], peer)

    src, inc, fin = (gw_half, gwc), (gw_yz, gwc_in), (gw_fin, gwc_fin)

    def gw_col(g, j):
        cc = (c + j) % 16
        return copy(src[g].at[cc if g else cc % 8], inc[g].at[j], gwy_s.at[g], gwy_r.at[g],
                    {"row": r, "col": cc, "depth": zh})

    def gw_all(g, j):
        return copy(fin[g].at[0], fin[g].at[j], gwf_s.at[g], gwf_r.at[g],
                    {"row": (r + j) % 8, "col": c, "depth": zh})

    def gw_col_wait(g):
        ref = inc[g].at[pl.ds(1, 15)]
        return copy(ref, ref, gwy_s.at[g], gwy_r.at[g], peer)

    def gw_all_wait(g):
        ref = fin[g].at[pl.ds(1, 7)]
        return copy(ref, ref, gwf_s.at[g], gwf_r.at[g], peer)

    def gw_send(q):
        @pl.loop(0, 7)
        def _(i):
            gw_row(q, far8(i)).start()

    def gw_sum(q):
        gw_rows(q).wait_recv()
        v = gw[q][x, k]
        for j in range(1, 8):
            v = v + gw_in[q][j]
        gw_half[:, q] = v.reshape(8, 8, BLK)
        if q == Q - 2:
            @pl.loop(0, 15)
            def _(i):
                gw_col(0, far16(i)).start()

    def gw_cols(g):
        gw_col_wait(g).wait_recv()
        v = src[g][c if g else c % 8]
        for j in range(1, 16):
            v = v + inc[g][j]
        if g == 0:
            v = jnp.concatenate([jnp.where(c < 8, v[..., :64], v[..., 64:])] * 2, axis=2)
        fin[g][0] = v

        @pl.loop(0, 7)
        def _(i):
            gw_all(g, far8(i)).start()

    def gw_end(g):
        gw_all_wait(g).wait_recv()
        if g == 0:
            for rr in range(8):
                v = fin[0][(r - rr + 8) % 8]
                for q in range(Q - 1):
                    for zz in range(2):
                        lane = (rr // 2 * 2 + zz) * BLK + START[q]
                        gw_out[rr % 2 * 8:rr % 2 * 8 + 8, lane:lane + 32] = v[q, :, zz * 32:(zz + 1) * 32]
        else:
            v = fin[1][r]
            for rr in range(1, 8):
                v = v + fin[1][(r - rr + 8) % 8]
            n = CHUNKS[-1]
            for kk in range(2):
                for zz in range(8):
                    lane = zz * BLK + START[-1]
                    gw_out[kk * 8:(kk + 1) * 8, lane:lane + n] = v[kk, :, zz * n:(zz + 1) * n]

    def early():
        for cp in pending:
            cp.wait_send()
        pending.clear()
        blk_done()
        for q in range(Q - 1):
            gw_rows(q).wait_send()

    def drain():
        last = pltpu.make_async_copy(gw_out, gw_hbm, loc.at[8])
        last.start()
        for cp in pending:
            cp.wait_send()
        for g in range(2):
            gw_col_wait(g).wait_send()
            gw_all_wait(g).wait_send()
        pltpu.make_async_copy(gf_out, gf_hbm, loc.at[7]).wait()
        last.wait()

    order = [
        (swap_send, 0), (y_first, 0, 0), (swap_send, 1), (swap_send, 2), (swap_send, 3), (blk_send,),
        (swap_wait, 0), (y_first, 0, 1), (y_first, 1, 0), (swap_wait, 1), (swap_wait, 2), (y_first, 1, 1),
        (tab_make,), (y_step, 0, 1, 0), (swap_wait, 3), (prep_w,), (y_step, 0, 1, 1), (y_step, 1, 1, 0),
        (y_step, 1, 1, 1), (y_step, 0, 2, 0), (prep_own,), (y_step, 0, 2, 1), (y_step, 1, 2, 0),
        (y_step, 1, 2, 1), (y_first, 2, 0), (y_step, 0, 3, 1), (y_step, 0, 3, 0), (y_first, 2, 1),
        (y_step, 1, 3, 0), (y_step, 1, 3, 1), (y_step, 2, 1, 0), (y_step, 0, 4, 1), (y_step, 0, 4, 0),
        (y_first, 3, 0), (spmm, 0, 0), (core_send, 0, 0), (y_step, 2, 1, 1), (y_first, 3, 1), (y_step, 1, 4, 0),
        (y_step, 1, 4, 1), (spmm, 1, 0), (y_step, 2, 2, 0), (core_send, 1, 0), (prep_peer,), (x_far, 0, 0),
        (y_step, 3, 1, 0), (spmm, 1, 1), (y_step, 2, 2, 1), (x_near, 0, 0), (core_send, 1, 1),
        (y_step, 3, 1, 1), (x_far, 1, 0), (spmm, 0, 1), (x_near, 1, 0), (y_step, 3, 2, 0), (y_step, 2, 3, 0),
        (core_send, 0, 1), (x_far, 1, 1), (y_step, 2, 3, 1), (z_start, 0, 0), (x_near, 1, 1), (x_far, 0, 1),
        (y_step, 3, 2, 1), (prep_feat,), (y_step, 3, 3, 0), (z_start, 1, 0), (x_near, 0, 1), (y_step, 2, 4, 0),
        (y_step, 2, 4, 1), (spmm, 2, 0), (core_send, 2, 0), (z_start, 1, 1), (y_step, 3, 3, 1), (z_two, 0),
        (spmm, 2, 1), (x_far, 2, 0), (y_step, 3, 4, 0), (z_start, 0, 1), (x_near, 2, 0), (z_two, 1),
        (core_send, 2, 1), (z_near, 1), (y_step, 3, 4, 1), (spmm, 3, 0), (core_send, 3, 0), (x_far, 2, 1),
        (spmm, 3, 1), (z_start, 2, 0), (x_near, 2, 1), (z_near, 0), (x_far, 3, 0), (core_send, 3, 1),
        (x_near, 3, 0), (x_far, 3, 1), (z_start, 2, 1), (x_near, 3, 1), (z_two, 2), (z_start, 3, 0),
        (z_start, 3, 1), (z_end, 0), (z_end, 1), (z_near, 2), (gw_dot, 0), (gf, 0), (z_two, 3), (z_near, 3),
        (gw_dot, 1), (z_end, 2), (gw_dot, 2), (gf, 1), (z_end, 3), (gw_dot, 3), (gw_sum, 0), (gw_sum, 1),
        (gf, 2), (early,), (gf, 3), (gw_sum, 2), (gw_cols, 1), (gw_cols, 0), (gw_end, 1), (gw_end, 0), (drain,),
    ]
    for fn, *args in order:
        fn(*args)


def finish(gft_hbm, gw_hbm, gf_out, gw_out, gft, gf, gw, sem):
    a = pltpu.make_async_copy(gft_hbm, gft, sem.at[0])
    b = pltpu.make_async_copy(gw_hbm, gw, sem.at[1])
    a.start()
    b.start()
    a.wait()
    for i in range(3):
        for h in range(2):
            gf[i * BLK:(i + 1) * BLK, h * BLK:(h + 1) * BLK] = gft[h * BLK:(h + 1) * BLK, i * BLK:(i + 1) * BLK].T
    c = pltpu.make_async_copy(gf, gf_out, sem.at[2])
    c.start()
    b.wait()
    d = pltpu.make_async_copy(gw, gw_out, sem.at[3])
    d.start()
    c.wait()
    d.wait()


def body(upstream, preact, features, weight, blocks, block_pos, block_count):
    vmem = pl.BlockSpec(memory_space=pltpu.VMEM)
    smem = pl.BlockSpec(memory_space=pltpu.SMEM)
    hbm = pl.BlockSpec(memory_space=pl.ANY)
    dma = pltpu.SemaphoreType.DMA
    V = pltpu.VMEM
    scratch = [
        V((384, 256), F32), V((384, 256), F32),
        V((256, 384), F32), V((16, 1024), F32),
        V((2, 3, BLK, BLK), F32),
        V((8, BLK), jnp.int32), pltpu.SMEM((8, BLK), jnp.int32),
        V((8, BLK), jnp.int32), pltpu.SMEM((8, BLK), jnp.int32),
        V((32, BLK, BLK), F32), V((32, BLK, BLK), F32),
        V((2, 32, BLK, BLK), BF16), V((2, 32, BLK, BLK), BF16),
        V((32, max(CHUNKS), BLK), F32),
        V((384, 256), F32), V((256, 1024), F32),
        V((256, 384), BF16), V((256, 384), BF16),
        V((256, 384), F32),
        V((16, 2, 8, 8 * CHUNKS[-1]), F32), V((16, 2, 8, 8 * CHUNKS[-1]), F32), V((8, 2, 8, 8 * CHUNKS[-1]), F32),
        V((8, Q - 1, 8, BLK), F32), V((16, Q - 1, 8, BLK), F32), V((8, Q - 1, 8, BLK), F32),
    ]
    for shape, dtype in (
        (lambda f: (48, f, BLK), F32), (lambda f: (4, 2, 2, 3, f, BLK), F32), (lambda f: (4, 2, 3, f, BLK), F32),
        (lambda f: (2, 3, 3, f, BLK), F32),
        (lambda f: (8 * f, 384), F32), (lambda f: (f, 384), F32),
        (lambda f: (8 * f, 384), BF16), (lambda f: (8 * f, 384), BF16),
        (lambda f: (256, 8 * f), BF16), (lambda f: (256, 8 * f), BF16),
        (lambda f: (4, 2, 2 * f, BLK), F32), (lambda f: (8, 2 * f, BLK), F32),
    ):
        scratch += [V(shape(f), dtype) for f in CHUNKS]
    scratch += [
        dma((9,)), dma((Q,)), dma((Q,)), dma((1,)), dma((1,)), dma((4,)), dma((4,)),
        dma((Q, 2, 2, 4)), dma((Q, 2, 2, 4)), dma((Q, 2, 4)), dma((Q, 2, 4)),
        dma((Q, 2, 3)), dma((Q, 2, 3)), dma((Q, 8)), dma((Q, 8)),
        dma((Q,)), dma((Q,)), dma((2,)), dma((2,)), dma((2,)), dma((2,)),
    ]
    turned_gf, gw = pl.pallas_call(
        kernel,
        out_shape=(jax.ShapeDtypeStruct((256, 384), F32), jax.ShapeDtypeStruct((16, 1024), F32)),
        in_specs=[hbm, hbm, vmem, smem, hbm, hbm, hbm],
        out_specs=(hbm, hbm),
        scratch_shapes=scratch,
        compiler_params=pltpu.CompilerParams(
            collective_id=0, has_side_effects=True, vmem_limit_bytes=56 * 2**20),
        cost_estimate=pl.CostEstimate(flops=2 * 10**9, bytes_accessed=6 * 2**20, transcendentals=0),
        name="graph_backward",
    )(upstream, preact, block_pos, block_count, features, weight, blocks.reshape(blocks.shape[2:]))
    return pl.pallas_call(
        finish,
        out_shape=(jax.ShapeDtypeStruct((384, 256), F32), jax.ShapeDtypeStruct((16, 1024), F32)),
        in_specs=[hbm, hbm], out_specs=(hbm, hbm),
        scratch_shapes=[V((256, 384), F32), V((384, 256), F32), V((16, 1024), F32), dma((4,))],
        compiler_params=pltpu.CompilerParams(vmem_limit_bytes=56 * 2**20),
        name="finish",
    )(turned_gf, gw)


def solution(mesh):
    in_specs = (
        P(("row", "col"), "depth"),
        P(("row", "col"), "depth"),
        P(("col", "row"), "depth"),
        P("depth", None),
        P("row", "col", None, None, None),
        P("row", "col", None),
        P("row", "col"),
    )
    out_specs = (P(("col", "row"), "depth"), P(("depth", "col"), None))
    return jax.shard_map(body, mesh=mesh, in_specs=in_specs, out_specs=out_specs, check_vma=False)
```

```python
import jax
import jax.numpy as jnp
from jax import lax
from jax.experimental import pallas as pl
from jax.experimental.pallas import tpu as pltpu
from jax.sharding import PartitionSpec as P

BLK = 128
CHUNKS = (32, 32, 32, 32)
Q = len(CHUNKS)
START = tuple(sum(CHUNKS[:q]) for q in range(Q))
MESH = pl.DeviceIdType.MESH
F32 = jnp.float32
BF16 = jnp.bfloat16
NT = (((1,), (1,)), ((), ()))


def split(v):
    hi = v.astype(BF16)
    return hi, (v - hi.astype(F32)).astype(BF16)


def dot(a, b):
    return jnp.dot(a, b, preferred_element_type=F32)


def dot_nt(a, b):
    return lax.dot_general(a, b, NT, preferred_element_type=F32)


def dot3(ah, al, bh, bl, f):
    return f(ah, bh) + f(al, bh) + f(ah, bl)


def down(row):
    return jnp.broadcast_to(row, (BLK, BLK)).T


def tables(pos, count):
    lane = lax.broadcasted_iota(jnp.int32, (1, BLK), 1)
    ii = lax.broadcasted_iota(jnp.int32, (BLK, BLK), 0)
    jj = lax.broadcasted_iota(jnp.int32, (BLK, BLK), 1)
    live = (lane < count).astype(jnp.int32)
    brow = (pos * 2731) >> 16
    col = jnp.where(live > 0, pos - 24 * brow, 24)
    col_i = down(col)
    key = col * BLK + lane
    rank = jnp.sum((down(key) < key).astype(jnp.int32), axis=0, keepdims=True)
    same = (col_i == col).astype(jnp.int32)
    seen = jnp.sum(same * (ii < jj).astype(jnp.int32), axis=0, keepdims=True)
    more = jnp.sum(same * (ii > jj).astype(jnp.int32), axis=0, keepdims=True)
    cont = jnp.where(seen > 0, live, 0)
    rank_i = down(rank)
    hot = (rank_i == jj).astype(jnp.int32)

    def put(v):
        return jnp.sum(hot * v, axis=0, keepdims=True)

    at_col = (col_i == jj).astype(jnp.int32)
    last = jnp.sum(at_col * down(jnp.where(more > 0, 0, rank)), axis=0, keepdims=True)
    has = (jnp.sum(at_col, axis=0, keepdims=True) > 0).astype(jnp.int32)
    return [put(down(brow)), put(ii), put(down(live)), put(down(cont)), last, has]


def kernel(up_hbm, pre_hbm, pos, count, feat_hbm, w_hbm, blk_hbm, gf_hbm, gw_hbm,
           up, pre, gf_out, gw_out, turned, tab_v, tab_own, peer_tab_v, peer_tab, own_blk, peer_blk, blk_hi, blk_lo, run,
           feat, wv, ft_hi, ft_lo, gft, *rest):
    gwc, gwc_in, gwc_fin, gw_half, gw_yz, gw_fin, *rest = rest
    parts = [rest[i * Q:(i + 1) * Q] for i in range(12)]
    (sig, part, core_in, near_in, back, other, back_hi, back_lo, w_hi, w_lo,
     gw, gw_in) = parts
    (loc, swap_s, swap_r, tab_s, tab_r, blk_s, blk_r, y_s, y_r, core_s, core_r,
     near_s, near_r, z_s, z_r, gwr_s, gwr_r, gwy_s, gwy_r, gwf_s, gwf_r) = rest[12 * Q:]

    r = lax.axis_index("row")
    c = lax.axis_index("col")
    zh = lax.axis_index("depth")
    x, k = r // 2, r % 2
    y, zl = c // 2, c % 2
    z = zh * 2 + zl

    def at(dx=0, dk=0, dy=0, dz=0):
        zz = (z + dz + 8) % 8
        return {"row": ((x + dx + 4) % 4) * 2 + (k + dk) % 2,
                "col": ((y + dy + 8) % 8) * 2 + zz % 2, "depth": zz // 2}

    peer = {"row": r, "col": y * 2 + 1 - zl, "depth": zh}
    pending = []

    def copy(src, dst, ssem, rsem, dev):
        return pltpu.make_async_remote_copy(src_ref=src, dst_ref=dst, send_sem=ssem, recv_sem=rsem,
                                            device_id=dev, device_id_type=MESH)

    def send(src, dst, ssem, rsem, dev):
        cp = copy(src, dst, ssem, rsem, dev)
        cp.start()
        pending.append(cp)

    def got(dst, ssem, rsem):
        copy(dst, dst, ssem, rsem, peer).wait_recv()

    local = [pltpu.make_async_copy(s, d, loc.at[i]) for i, (s, d) in enumerate(
        ((blk_hbm, own_blk), (feat_hbm, feat), (w_hbm, wv), (up_hbm, up), (pre_hbm, pre)))]
    local[3].start()
    local[4].start()

    bar = pltpu.get_barrier_semaphore()
    for dev in (at(dx=2), at(dx=1), at(dx=-1), at(dk=1), at(dy=1), at(dy=-1), at(dz=1), at(dz=-1), at(dz=2), at(dz=-2)):
        pl.semaphore_signal(bar, inc=1, device_id=dev, device_id_type=MESH)

    local[3].wait()
    local[4].wait()

    for i in range(3):
        for h in range(2):
            u = up[i * BLK:(i + 1) * BLK, h * BLK:(h + 1) * BLK]
            p = pre[i * BLK:(i + 1) * BLK, h * BLK:(h + 1) * BLK]
            turned[h, i] = (u * (p > 0).astype(F32)).T
    for i in range(3):
        v = turned[zl, i]
        for q in range(Q):
            sig[q][6 * y + 3 * zl + i] = v[START[q]:START[q] + CHUNKS[q]]

    for cp in local[:3]:
        cp.start()

    pl.semaphore_wait(bar, 10)

    n_slots = jnp.where(r == 0, 32, 16)

    def swap_send(q):
        send(turned.at[1 - zl, :, pl.ds(START[q], CHUNKS[q])], sig[q].at[pl.ds(6 * y + 3 * zl, 3)],
             swap_s.at[q], swap_r.at[q], peer)

    def swap_wait(q):
        got(sig[q].at[pl.ds(6 * y + 3 * (1 - zl), 3)], swap_s.at[q], swap_r.at[q])

    def y_piece(q, yo, hr):
        h = zl if hr == 0 else 1 - zl
        return sig[q].at[pl.ds(6 * yo + 3 * h, 3)]

    def y_send(q, d, s, hr):
        sgn = 1 - 2 * d
        ref = y_piece(q, (y - sgn * (s - 1) + 8) % 8, hr)
        send(ref, ref, y_s.at[q, d, hr, s - 1], y_r.at[q, d, hr, s - 1], at(dy=sgn))

    def y_first(q, hr):
        for d in range(2):
            y_send(q, d, 1, hr)

    def y_step(q, s, hr):
        for d in range(2):
            last = 4 if d == hr else 3
            if s > last:
                continue
            sgn = 1 - 2 * d
            got(y_piece(q, (y - sgn * s + 8) % 8, hr), y_s.at[q, d, hr, s - 1], y_r.at[q, d, hr, s - 1])
            if s < last:
                y_send(q, d, s + 1, hr)

    def blk_copy(j):
        lo = 8 * j
        return copy(blk_hbm.at[pl.ds(lo, 8)], peer_blk.at[pl.ds(lo, 8)], blk_s.at[j], blk_r.at[j],
                    at(dz=1 if j % 2 == 0 else -1))

    def tab_make():
        tab_v[...] = jnp.zeros_like(tab_v)
        tab_v[0:1, 0:32] = pos[0]
        for i, v in enumerate(tables(tab_v[0:1], count[0, 0])):
            tab_v[i:i + 1] = v
        send(tab_v, peer_tab_v, tab_s.at[0], tab_r.at[0], peer)
        cp = pltpu.make_async_copy(tab_v, tab_own, loc.at[5])
        cp.start()
        cp.wait()

    def blk_send():
        for j in range(2):
            blk_copy(j).start()

        @pl.when(r == 0)
        def _():
            for j in range(2, 4):
                blk_copy(j).start()

    def blk_wait():
        for j in range(2):
            blk_copy(j).wait_recv()

        @pl.when(r == 0)
        def _():
            for j in range(2, 4):
                blk_copy(j).wait_recv()

    def blk_done():
        for j in range(2):
            blk_copy(j).wait_send()

        @pl.when(r == 0)
        def _():
            for j in range(2, 4):
                blk_copy(j).wait_send()

    def split_blocks(rel):
        src = own_blk if rel == 0 else peer_blk

        @pl.loop(0, n_slots)
        def _(i):
            hi, lo = split(src[i])
            blk_hi[rel, i] = hi
            blk_lo[rel, i] = lo

    def prep_own():
        local[0].wait()
        split_blocks(0)

    def prep_peer():
        got(peer_tab_v, tab_s.at[0], tab_r.at[0])
        cp = pltpu.make_async_copy(peer_tab_v, peer_tab, loc.at[3])
        cp.start()
        blk_wait()
        split_blocks(1)
        cp.wait()

    def prep_feat():
        local[1].wait()
        for i in range(3):
            for h in range(2):
                t = feat[i * BLK:(i + 1) * BLK, h * BLK:(h + 1) * BLK].T
                t = t.reshape(8, 2, 8, BLK)
                for kk in range(2):
                    hi, lo = split(t[:, kk].reshape(64, BLK))
                    row = kk * BLK + h * 64
                    ft_hi[row:row + 64, i * BLK:(i + 1) * BLK] = hi
                    ft_lo[row:row + 64, i * BLK:(i + 1) * BLK] = lo

    def prep_w():
        local[2].wait()
        for q in range(Q):
            lo, n = START[q], CHUNKS[q]
            v = jnp.concatenate([wv[:, zz * BLK + lo:zz * BLK + lo + n] for zz in range(8)], axis=1)
            w_hi[q][...], w_lo[q][...] = split(v)

    def spmm(q, rel):
        tab = tab_own if rel == 0 else peer_tab
        f = CHUNKS[q]

        def step(it, acc):
            terms = []
            for u in range(4):
                i = it * 4 + u
                sh, sl = split(sig[q][tab[0, i]])
                o = tab[1, i]
                t = dot(jnp.concatenate([sh, sl], axis=0), blk_hi[rel, o])
                t = t[:f] + t[f:] + dot(sh, blk_lo[rel, o])
                terms.append(t * tab[2, i].astype(F32))
            for u in range(4):
                i = it * 4 + u
                acc = terms[u] + acc * tab[3, i].astype(F32)
                run[i, 0:f] = acc
            return acc

        lax.fori_loop(0, n_slots // 4, step, jnp.zeros((f, BLK), F32))
        for b in range(24):
            rr = b // 3
            part[q][rr // 2, rr % 2, rel, b % 3] = run[tab[4, b], 0:f] * tab[5, b].astype(F32)

    def core_send(q, rel):
        for o in (2, 1, 3, 0):
            xx = (x + o) % 4
            send(part[q].at[xx, 1 - k, rel], core_in[q].at[xx, rel],
                 core_s.at[q, rel, o], core_r.at[q, rel, o], at(dk=1))

    def core_sum(q, rel, o):
        xx = (x + o) % 4
        got(core_in[q].at[xx, rel], core_s.at[q, rel, o], core_r.at[q, rel, o])
        part[q][xx, k, rel] = part[q][xx, k, rel] + core_in[q][xx, rel]

    def x_send(q, rel, o):
        core_sum(q, rel, o)
        send(part[q].at[(x + o) % 4, k, rel], near_in[q].at[rel, o - 1],
             near_s.at[q, rel, o - 1], near_r.at[q, rel, o - 1], at(dx=o))

    def x_far(q, rel):
        x_send(q, rel, 2)

    def x_near(q, rel):
        x_send(q, rel, 1)
        x_send(q, rel, 3)
        core_sum(q, rel, 0)

    def z_piece(q, dz):
        return back[q].at[pl.ds(((z + dz + 8) % 8) * CHUNKS[q], CHUNKS[q])]

    def z_half(q, dz, d):
        f = CHUNKS[q] // 2
        return back[q].at[pl.ds(((z + dz + 8) % 8) * 2 * f + d * f, f)]

    def z_start(q, rel):
        for h in range(3):
            got(near_in[q].at[rel, h], near_s.at[q, rel, h], near_r.at[q, rel, h])
        for i in range(3):
            v = (part[q][x, k, rel, i] + near_in[q][rel, 0, i]) + (near_in[q][rel, 1, i] + near_in[q][rel, 2, i])
            if rel == 0:
                back[q][pl.ds(z * CHUNKS[q], CHUNKS[q]), i * BLK:(i + 1) * BLK] = v
            else:
                other[q][:, i * BLK:(i + 1) * BLK] = v
        for d, sgn in ((0, 1), (1, -1)):
            if rel == 0:
                send(z_piece(q, 0), z_piece(q, 0), z_s.at[q, 2 + d], z_r.at[q, 2 + d], at(dz=2 * sgn))
            else:
                send(other[q], z_piece(q, 0), z_s.at[q, d], z_r.at[q, d], at(dz=sgn))

    def z_near(q):
        for d, sgn in ((0, 1), (1, -1)):
            ref = z_piece(q, -sgn)
            got(ref, z_s.at[q, d], z_r.at[q, d])
            send(ref, ref, z_s.at[q, 4 + d], z_r.at[q, 4 + d], at(dz=2 * sgn))

    def z_two(q):
        for d, sgn in ((0, 1), (1, -1)):
            got(z_piece(q, -2 * sgn), z_s.at[q, 2 + d], z_r.at[q, 2 + d])
            ref = z_half(q, -2 * sgn, d)
            send(ref, ref, z_s.at[q, 6 + d], z_r.at[q, 6 + d], at(dz=2 * sgn))

    def z_end(q):
        for d, sgn in ((0, 1), (1, -1)):
            got(z_piece(q, -3 * sgn), z_s.at[q, 4 + d], z_r.at[q, 4 + d])
        for d, sgn in ((0, 1), (1, -1)):
            got(z_half(q, -4 * sgn, d), z_s.at[q, 6 + d], z_r.at[q, 6 + d])

    def gw_dot(q):
        bh, bl = split(back[q][...])
        back_hi[q][...] = bh
        back_lo[q][...] = bl
        g = dot3(ft_hi[...], ft_lo[...], bh, bl, dot_nt)
        if q == Q - 1:
            for kk in range(2):
                gwc[:, kk] = g[kk * BLK:(kk + 1) * BLK].reshape(16, 8, 8 * CHUNKS[q])

            for i in range(15):
                gw_col(1, far16(i)).start()
            return
        w = 2 * CHUNKS[q]
        for xx in range(4):
            v = g[:, xx * w:(xx + 1) * w].reshape(2, BLK, w)
            if w < BLK:
                v = jnp.concatenate([v[:, :64], v[:, 64:]], axis=2)
            gw[q][xx] = v
        gw_send(q)

    def gf(q):
        t = dot3(w_hi[q][...], w_lo[q][...], back_hi[q][...], back_lo[q][...], dot)
        if q > 0:
            t = gft[...] + t
        if q < Q - 1:
            gft[...] = t
        else:
            gf_out[...] = t
            pltpu.make_async_copy(gf_out, gf_hbm, loc.at[7]).start()

    def far8(i):
        return 4 + (1 - 2 * (i % 2)) * ((i + 1) // 2)

    def far16(i):
        return 8 + (1 - 2 * (i % 2)) * ((i + 1) // 2)

    def gw_row(q, j):
        rr = (r + j) % 8
        return copy(gw[q].at[rr // 2, rr % 2], gw_in[q].at[j], gwr_s.at[q], gwr_r.at[q],
                    {"row": rr, "col": c, "depth": zh})

    def gw_rows(q):
        ref = gw_in[q].at[pl.ds(1, 7)]
        return copy(ref, ref, gwr_s.at[q], gwr_r.at[q], peer)

    src, inc, fin = (gw_half, gwc), (gw_yz, gwc_in), (gw_fin, gwc_fin)

    def gw_col(g, j):
        cc = (c + j) % 16
        return copy(src[g].at[cc if g else cc % 8], inc[g].at[j], gwy_s.at[g], gwy_r.at[g],
                    {"row": r, "col": cc, "depth": zh})

    def gw_all(g, j):
        return copy(fin[g].at[0], fin[g].at[j], gwf_s.at[g], gwf_r.at[g],
                    {"row": (r + j) % 8, "col": c, "depth": zh})

    def gw_col_wait(g):
        ref = inc[g].at[pl.ds(1, 15)]
        return copy(ref, ref, gwy_s.at[g], gwy_r.at[g], peer)

    def gw_all_wait(g):
        ref = fin[g].at[pl.ds(1, 7)]
        return copy(ref, ref, gwf_s.at[g], gwf_r.at[g], peer)

    def gw_send(q):
        @pl.loop(0, 7)
        def _(i):
            gw_row(q, far8(i)).start()

    def gw_sum(q):
        gw_rows(q).wait_recv()
        v = gw[q][x, k]
        for j in range(1, 8):
            v = v + gw_in[q][j]
        gw_half[:, q] = v.reshape(8, 8, BLK)
        if q == Q - 2:
            for i in range(15):
                gw_col(0, far16(i)).start()

    def gw_cols(g):
        gw_col_wait(g).wait_recv()
        v = src[g][c if g else c % 8]
        for j in range(1, 16):
            v = v + inc[g][j]
        if g == 0:
            v = jnp.concatenate([jnp.where(c < 8, v[..., :64], v[..., 64:])] * 2, axis=2)
        fin[g][0] = v

        for i in range(7):
            gw_all(g, far8(i)).start()

    def gw_end(g):
        gw_all_wait(g).wait_recv()
        if g == 0:
            for rr in range(8):
                v = fin[0][(r - rr + 8) % 8]
                for q in range(Q - 1):
                    for zz in range(2):
                        lane = (rr // 2 * 2 + zz) * BLK + START[q]
                        gw_out[rr % 2 * 8:rr % 2 * 8 + 8, lane:lane + 32] = v[q, :, zz * 32:(zz + 1) * 32]
        else:
            v = fin[1][r]
            for rr in range(1, 8):
                v = v + fin[1][(r - rr + 8) % 8]
            n = CHUNKS[-1]
            for kk in range(2):
                for zz in range(8):
                    lane = zz * BLK + START[-1]
                    gw_out[kk * 8:(kk + 1) * 8, lane:lane + n] = v[kk, :, zz * n:(zz + 1) * n]

    def early():
        for cp in pending:
            cp.wait_send()
        pending.clear()
        blk_done()
        for q in range(Q - 1):
            gw_rows(q).wait_send()

    def drain():
        last = pltpu.make_async_copy(gw_out, gw_hbm, loc.at[8])
        last.start()
        for cp in pending:
            cp.wait_send()
        for g in range(2):
            gw_col_wait(g).wait_send()
            gw_all_wait(g).wait_send()
        pltpu.make_async_copy(gf_out, gf_hbm, loc.at[7]).wait()
        last.wait()

    order = [
        (swap_send, 0), (swap_send, 1), (y_first, 0, 0), (swap_send, 2), (swap_send, 3), (blk_send,),
        (swap_wait, 0), (y_first, 0, 1), (prep_own,), (tab_make,), (swap_wait, 1), (y_first, 1, 0),
        (y_step, 0, 1, 0), (y_first, 1, 1), (swap_wait, 2), (y_step, 0, 1, 1), (swap_wait, 3), (y_first, 2, 0),
        (y_step, 1, 1, 0), (y_step, 0, 2, 0), (y_step, 0, 2, 1), (prep_feat,), (y_step, 1, 1, 1),
        (y_first, 2, 1), (y_step, 0, 3, 0), (y_step, 0, 3, 1), (prep_w,), (y_step, 1, 2, 1), (y_step, 1, 2, 0),
        (y_step, 2, 1, 0), (y_step, 2, 1, 1), (y_step, 0, 4, 0), (y_step, 0, 4, 1), (spmm, 0, 0),
        (core_send, 0, 0), (y_step, 1, 3, 1), (y_first, 3, 0), (y_step, 1, 3, 0), (x_far, 0, 0),
        (y_first, 3, 1), (y_step, 2, 2, 0), (x_near, 0, 0), (prep_peer,), (y_step, 2, 2, 1), (spmm, 0, 1),
        (core_send, 0, 1), (y_step, 1, 4, 1), (y_step, 3, 1, 0), (y_step, 1, 4, 0), (spmm, 1, 1),
        (y_step, 3, 1, 1), (x_far, 0, 1), (z_start, 0, 0), (core_send, 1, 1), (x_near, 0, 1), (y_step, 2, 3, 0),
        (y_step, 2, 3, 1), (spmm, 1, 0), (x_far, 1, 1), (y_step, 3, 2, 0), (core_send, 1, 0), (x_near, 1, 1),
        (y_step, 3, 2, 1), (z_start, 0, 1), (y_step, 2, 4, 0), (x_far, 1, 0), (y_step, 2, 4, 1), (z_two, 0),
        (spmm, 2, 0), (y_step, 3, 3, 0), (x_near, 1, 0), (core_send, 2, 0), (y_step, 3, 3, 1), (z_start, 1, 1),
        (z_near, 0), (spmm, 2, 1), (core_send, 2, 1), (x_far, 2, 0), (y_step, 3, 4, 0), (x_near, 2, 0),
        (z_start, 1, 0), (y_step, 3, 4, 1), (spmm, 3, 0), (core_send, 3, 0), (x_far, 2, 1), (z_near, 1),
        (x_near, 2, 1), (spmm, 3, 1), (x_far, 3, 0), (core_send, 3, 1), (z_start, 2, 0), (x_near, 3, 0),
        (z_end, 0), (x_far, 3, 1), (z_two, 1), (z_start, 2, 1), (x_near, 3, 1), (z_start, 3, 0), (gw_dot, 0),
        (z_start, 3, 1), (gf, 0), (z_end, 1), (z_two, 2), (z_near, 2), (gw_dot, 1), (z_two, 3), (gf, 1),
        (z_near, 3), (gw_sum, 0), (gw_sum, 1), (z_end, 2), (gw_dot, 2), (gf, 2), (z_end, 3), (gw_dot, 3),
        (gf, 3), (early,), (gw_sum, 2), (gw_cols, 1), (gw_cols, 0), (gw_end, 1), (gw_end, 0), (drain,),
    ]
    for fn, *args in order:
        fn(*args)


def finish(gft_hbm, gw_hbm, gf_out, gw_out, gft, gf, gw, sem):
    into = [pltpu.make_async_copy(gft_hbm.at[:, pl.ds(i * BLK, BLK)], gft.at[:, pl.ds(i * BLK, BLK)], sem.at[i])
            for i in range(3)]
    into.append(pltpu.make_async_copy(gw_hbm, gw, sem.at[3]))
    out = [pltpu.make_async_copy(gf.at[pl.ds(i * BLK, BLK)], gf_out.at[pl.ds(i * BLK, BLK)], sem.at[4 + i])
           for i in range(3)]
    out.append(pltpu.make_async_copy(gw, gw_out, sem.at[7]))
    for cp in into:
        cp.start()
    for i in range(3):
        into[i].wait()
        for h in range(2):
            gf[i * BLK:(i + 1) * BLK, h * BLK:(h + 1) * BLK] = gft[h * BLK:(h + 1) * BLK, i * BLK:(i + 1) * BLK].T
        out[i].start()
    into[3].wait()
    out[3].start()
    for cp in out:
        cp.wait()


def body(upstream, preact, features, weight, blocks, block_pos, block_count):
    vmem = pl.BlockSpec(memory_space=pltpu.VMEM)
    smem = pl.BlockSpec(memory_space=pltpu.SMEM)
    hbm = pl.BlockSpec(memory_space=pl.ANY)
    dma = pltpu.SemaphoreType.DMA
    V = pltpu.VMEM
    scratch = [
        V((384, 256), F32), V((384, 256), F32),
        V((256, 384), F32), V((16, 1024), F32),
        V((2, 3, BLK, BLK), F32),
        V((8, BLK), jnp.int32), pltpu.SMEM((8, BLK), jnp.int32),
        V((8, BLK), jnp.int32), pltpu.SMEM((8, BLK), jnp.int32),
        V((32, BLK, BLK), F32), V((32, BLK, BLK), F32),
        V((2, 32, BLK, BLK), BF16), V((2, 32, BLK, BLK), BF16),
        V((32, max(CHUNKS), BLK), F32),
        V((384, 256), F32), V((256, 1024), F32),
        V((256, 384), BF16), V((256, 384), BF16),
        V((256, 384), F32),
        V((16, 2, 8, 8 * CHUNKS[-1]), F32), V((16, 2, 8, 8 * CHUNKS[-1]), F32), V((8, 2, 8, 8 * CHUNKS[-1]), F32),
        V((8, Q - 1, 8, BLK), F32), V((16, Q - 1, 8, BLK), F32), V((8, Q - 1, 8, BLK), F32),
    ]
    for shape, dtype in (
        (lambda f: (48, f, BLK), F32), (lambda f: (4, 2, 2, 3, f, BLK), F32), (lambda f: (4, 2, 3, f, BLK), F32),
        (lambda f: (2, 3, 3, f, BLK), F32),
        (lambda f: (8 * f, 384), F32), (lambda f: (f, 384), F32),
        (lambda f: (8 * f, 384), BF16), (lambda f: (8 * f, 384), BF16),
        (lambda f: (256, 8 * f), BF16), (lambda f: (256, 8 * f), BF16),
        (lambda f: (4, 2, 2 * f, BLK), F32), (lambda f: (8, 2 * f, BLK), F32),
    ):
        scratch += [V(shape(f), dtype) for f in CHUNKS]
    scratch += [
        dma((9,)), dma((Q,)), dma((Q,)), dma((1,)), dma((1,)), dma((4,)), dma((4,)),
        dma((Q, 2, 2, 4)), dma((Q, 2, 2, 4)), dma((Q, 2, 4)), dma((Q, 2, 4)),
        dma((Q, 2, 3)), dma((Q, 2, 3)), dma((Q, 8)), dma((Q, 8)),
        dma((Q,)), dma((Q,)), dma((2,)), dma((2,)), dma((2,)), dma((2,)),
    ]
    turned_gf, gw = pl.pallas_call(
        kernel,
        out_shape=(jax.ShapeDtypeStruct((256, 384), F32), jax.ShapeDtypeStruct((16, 1024), F32)),
        in_specs=[hbm, hbm, vmem, smem, hbm, hbm, hbm],
        out_specs=(hbm, hbm),
        scratch_shapes=scratch,
        compiler_params=pltpu.CompilerParams(
            collective_id=0, has_side_effects=True, vmem_limit_bytes=56 * 2**20),
        cost_estimate=pl.CostEstimate(flops=2 * 10**9, bytes_accessed=6 * 2**20, transcendentals=0),
        name="graph_backward",
    )(upstream, preact, block_pos, block_count, features, weight, blocks.reshape(blocks.shape[2:]))
    return pl.pallas_call(
        finish,
        out_shape=(jax.ShapeDtypeStruct((384, 256), F32), jax.ShapeDtypeStruct((16, 1024), F32)),
        in_specs=[hbm, hbm], out_specs=(hbm, hbm),
        scratch_shapes=[V((256, 384), F32), V((384, 256), F32), V((16, 1024), F32), dma((8,))],
        compiler_params=pltpu.CompilerParams(vmem_limit_bytes=56 * 2**20),
        name="finish",
    )(turned_gf, gw)


def solution(mesh):
    in_specs = (
        P(("row", "col"), "depth"),
        P(("row", "col"), "depth"),
        P(("col", "row"), "depth"),
        P("depth", None),
        P("row", "col", None, None, None),
        P("row", "col", None),
        P("row", "col"),
    )
    out_specs = (P(("col", "row"), "depth"), P(("depth", "col"), None))
    return jax.shard_map(body, mesh=mesh, in_specs=in_specs, out_specs=out_specs, check_vma=False)
```
